512 devices in a mesh: seq: 32 (over y, z_hi, core), chan: 16 (over x, z_lo).
Axes of the slice: x: 4, y: 8, z: 8 (z_hi: 2, z_lo: 4; z = z_hi * 4 + z_lo), core: 2. Of those that a mesh axis runs over, the one named last changes fastest.
Arguments:
- projected: bfloat16 [16384, 3, 4096], P('seq', None, 'chan'), may hold values from -6 to 6
- short_w: float32 [3, 3, 4096], P(None, None, 'chan'), may hold values from -3.5 to 3.5
- residues: float32 [4096, 16], P('chan'), may hold values from -1.5 to 1.5
- rates: float32 [4096, 16], P('chan'), may hold values from 0.5 to 500
- skip: float32 [4096], P('chan'), may hold values from 0.5 to 1.5
- w_out: bfloat16 [4096, 8192], P('seq', 'chan'), may hold values from -0.09375 to 0.09375
Outputs:
- layer_out: bfloat16 [16384, 8192], P('seq', 'chan')
The draws below stay inside these ranges and needn't reach their ends.
All inputs are finite; a program needn't handle non-finite values.
Results may differ from the reference program's by a relative error of at most 0.015.
Values may be sent and summed in bfloat16 or wider, within the bound.
A program may use at most 64 MiB of HBM per device.

```python
import math
import jax
import jax.numpy as jnp
from jax import lax

D = 8192
C = 4096
MODES = 16
TAPS = 3
L = 16384


def shard_levels(key, shape, cuts, least, largest):
    factor_of, own = 1.0, jax.random.fold_in(key, 6)
    for dim, parts in cuts:
        heights = jnp.exp(jax.random.uniform(jax.random.fold_in(own, dim), (parts,), jnp.float32, least / len(cuts), largest / len(cuts)))
        factor_of = factor_of * jnp.repeat(heights, shape[dim] // parts).reshape([-1 if axis == dim else 1 for axis in range(len(shape))])
    return factor_of


def centred(key, dims, scale, most, shards=(), kind=jnp.bfloat16):
    values = scale * jax.random.normal(key, dims, jnp.float32)
    if shards:
        values = values * shard_levels(key, dims, shards, -0.22, 0.18)
    return jnp.clip(values, -most, most).astype(kind)


def setup_inputs(seed: int = 0) -> dict:
    seeds = jax.random.split(jax.random.key(seed), 7)
    projected = centred(seeds[0], (L, 3, C), 1.0, 6.0, ((0, 32), (2, 16)))
    short_w = centred(seeds[1], (TAPS, 3, C), TAPS ** -0.5, 3.5, ((2, 16),), jnp.float32)
    residues = centred(seeds[2], (C, MODES), 0.25, 1.5, ((0, 16),), jnp.float32)
    rates = jnp.clip(jnp.exp(math.log(500.0) - 6.9077553 * jax.random.uniform(seeds[3], (C, MODES), jnp.float32) ** shard_levels(seeds[3], (C, MODES), ((0, 16),), -0.2, 0.2)), 0.5, 500.0)
    skip = jnp.clip(0.5 + 1.0 * jax.random.uniform(seeds[4], (C,), jnp.float32) ** shard_levels(seeds[4], (C,), ((0, 16),), -0.2, 0.2), 0.5, 1.5)
    w_out = centred(seeds[5], (C, D), C ** -0.5, 0.09375, ((0, 32), (1, 16)))
    return {"projected": projected, "short_w": short_w, "residues": residues, "rates": rates, "skip": skip, "w_out": w_out}


def filter_block(res_block, rate_block, length):
    times = jnp.arange(length).astype(jnp.float32) / length
    scale = res_block * jnp.sqrt(2.0 * rate_block / length)
    decays = jnp.exp(-rate_block[:, :, None] * times[None, None, :])
    return lax.optimization_barrier(jnp.sum(scale[:, :, None] * decays, axis=1))

def reference(projected, short_w, residues, rates, skip, w_out):
    values = projected.astype(jnp.float32)
    padded = jnp.pad(values, ((2, 0), (0, 0), (0, 0)))
    feat = short_w[0] * padded[2:] + short_w[1] * padded[1:-1] + short_w[2] * padded[:-2]
    query = feat[:, 0, :].astype(jnp.bfloat16)
    inner = (feat[:, 1, :] * feat[:, 2, :]).astype(jnp.bfloat16)
    blocks = C // 128
    inner_blocks = inner.T.reshape(blocks, 128, L)
    res_blocks = residues.reshape(blocks, 128, MODES)
    rate_blocks = rates.reshape(blocks, 128, MODES)
    skip_blocks = skip.reshape(blocks, 128)

    def one_block(items):
        signal, res_block, rate_block, skip_block = items
        filt = filter_block(res_block, rate_block, L)
        signal32 = signal.astype(jnp.float32)
        spec_u = jnp.fft.rfft(signal32, n=2 * L, axis=1)
        spec_h = jnp.fft.rfft(filt, n=2 * L, axis=1)
        conv = jnp.fft.irfft(spec_u * spec_h, n=2 * L, axis=1)[:, :L]
        return (conv + skip_block[:, None] * signal32).astype(jnp.bfloat16)
    conv = lax.map(one_block, (inner_blocks, res_blocks, rate_blocks, skip_blocks))
    conv = conv.reshape(C, L).T
    gated = (query.astype(jnp.float32) * conv.astype(jnp.float32)).astype(jnp.bfloat16)
    return jnp.dot(gated, w_out, preferred_element_type=jnp.float32).astype(jnp.bfloat16)
```

```python
import functools

import jax
import jax.numpy as jnp
from jax import lax
from jax.experimental import pallas as pl
from jax.experimental.pallas import tpu as pltpu
from jax.sharding import PartitionSpec as P

MESH = pl.DeviceIdType.MESH
MODES = 16
SUBS = 8
LANES = 128
F32, BF16 = jnp.float32, jnp.bfloat16


def rounded(value):
    return value.astype(BF16).astype(F32)


def total_of(terms):
    terms = list(terms)
    while len(terms) > 1:
        terms = [a + b for a, b in zip(terms[::2], terms[1::2])] + terms[len(terms) // 2 * 2 :]
    return terms[0]


def kernel(
    length,
    proj,
    short_w,
    res,
    rate,
    skip,
    w_own,
    out,
    wide,
    coef,
    dec,
    sub_dec,
    u_buf,
    q_buf,
    y_buf,
    part,
    own_total,
    pair,
    msg,
    g_wide,
    g_all,
    w_all,
    acc,
    pair_sem,
    msg_send,
    msg_recv,
    w_send,
    w_recv,
    z_send,
    z_recv,
    x_send,
    x_recv,
):
    s = lax.axis_index("seq")
    c = lax.axis_index("chan")
    y, zh, k = s // 4, (s // 2) % 2, s % 2
    x, zl = c // 4, c % 4
    h = s // 2
    tokens, chans = proj.shape[1], proj.shape[2]
    tiles = chans // LANES
    steps = tokens // SUBS
    half = tokens // 2

    def seq_of(yy, zz, kk):
        return yy * 4 + zz * 2 + kk

    up_y, down_y = (y + 1) % 8, (y + 7) % 8
    right, left, across = (x + 1) % 4, (x + 3) % 4, (x + 2) % 4
    partner = seq_of(y, zh, 1 - k)

    barrier = pltpu.get_barrier_semaphore()

    def greet(seq, chan):
        pl.semaphore_signal(barrier, inc=1, device_id=(seq, chan), device_id_type=MESH)

    greet(partner, c)
    for step in (1, 3):
        greet(s, (x + step) % 4 * 4 + zl)
        greet(s, x * 4 + (zl + step) % 4)

    def greet_chip(step, _):
        greet((h + step) % 16 * 2 + k, c)
        return 0

    lax.fori_loop(1, 16, greet_chip, 0)

    speed = rate[...] * (1.0 / length)
    scale = res[...] * jnp.sqrt(2.0 * rate[...] * (1.0 / length))
    coef[...] = scale

    def decay(count):
        return jnp.exp(speed * (-1.0 * count))

    for at, count in enumerate((1, steps, 2 * steps, 4 * steps)):
        dec[at] = decay(count)
    sub = lax.broadcasted_iota(jnp.int32, (SUBS, chans), 0)
    sub_steps = sub.astype(F32) * (-1.0 * steps)
    for m in range(MODES):
        sub_dec[m] = jnp.exp(jnp.broadcast_to(speed[m : m + 1], (SUBS, chans)) * sub_steps)

    for stream in range(3):
        for tile in range(tiles):
            lanes = pl.ds(tile * LANES, LANES)
            wide[stream, tile, 0:8, :] = jnp.zeros((8, LANES), F32)
            wide[stream, tile, 8 : 8 + tokens, :] = proj[stream, :, lanes].astype(F32)

    sub1 = lax.broadcasted_iota(jnp.int32, (SUBS, LANES), 0)
    keep = jnp.where((sub1 > 0) | (s == 0), 1.0, 0.0).astype(F32)

    def row(ref, lanes, *index):
        return jnp.broadcast_to(ref[index + (lanes,)], (SUBS, LANES))

    for tile in range(tiles):
        lanes = pl.ds(tile * LANES, LANES)
        taps = [[row(short_w, lanes, j, slice(st, st + 1)) for j in range(3)] for st in range(3)]
        skip_row = row(skip, lanes, slice(0, 1))

        def rows_at(stream, start, tile=tile):
            return wide[stream, tile, pl.ds(start, SUBS, stride=steps), :]

        def scan_step(i, carry, first=False, tile=tile, lanes=lanes, taps=taps, skip_row=skip_row):
            state, behind = carry
            feats, now = [], []
            for st in range(3):
                value = rows_at(st, 8 + i)
                one, two = behind[st]
                feats.append(taps[st][0] * value + taps[st][1] * one + taps[st][2] * two)
                now.append((value, one))
            u = rounded(feats[1] * feats[2])
            if first:
                u = u * keep
            state = tuple(
                row(dec, lanes, 0, slice(m, m + 1)) * state[m] + row(coef, lanes, slice(m, m + 1)) * u
                for m in range(MODES)
            )
            q_buf[i, :, lanes] = rounded(feats[0])
            u_buf[i, :, lanes] = u
            y_buf[i, :, lanes] = total_of(state) + skip_row * u
            return state, tuple(now)

        carry = (
            tuple(jnp.zeros((SUBS, LANES), F32) for _ in range(MODES)),
            tuple((rows_at(st, 7), rows_at(st, 6)) for st in range(3)),
        )
        carry = scan_step(0, carry, True)
        carry = scan_step(1, carry, True)
        state, _ = lax.fori_loop(2, steps, scan_step, carry)
        for m in range(MODES):
            value = state[m]
            for at, shift in ((1, 1), (2, 2), (3, 4)):
                moved = pltpu.roll(value, shift, 0)
                value = value + row(dec, lanes, at, slice(m, m + 1)) * jnp.where(sub1 >= shift, moved, 0.0)
            own_total[m : m + 1, lanes] = value[SUBS - 1 : SUBS]
            part[m, :, lanes] = jnp.where(sub1 >= 1, pltpu.roll(value, 1, 0), 0.0)

    def ends(stream, first):
        start = 0 if first else tokens - 2
        return jnp.concatenate([wide[stream, t, pl.ds(8 + start, 2), :] for t in range(tiles)], axis=1)

    mine = [own_total[...]]
    mine += [ends(1, True), ends(2, True), ends(1, False), ends(2, False), ends(0, False)]
    mine += [jnp.zeros((6, chans), F32)]
    pair[0] = jnp.concatenate(mine, axis=0).astype(BF16)

    pl.semaphore_wait(barrier, 20)

    pair_copy = pltpu.make_async_remote_copy(
        src_ref=pair.at[0], dst_ref=pair.at[1], send_sem=pair_sem.at[0], recv_sem=pair_sem.at[1],
        device_id=(partner, c), device_id_type=MESH,
    )
    pair_copy.start()

    def w_copy(slot, at, seq):
        return pltpu.make_async_remote_copy(
            src_ref=w_all.at[slot], dst_ref=w_all.at[slot], send_sem=w_send.at[at], recv_sem=w_recv.at[slot],
            device_id=(seq, c), device_id_type=MESH,
        )

    w_started = []

    def w_go(slot, seq):
        copy = w_copy(slot, len(w_started), seq)
        copy.start()
        w_started.append(copy)

    def w_here(slot):
        w_copy(slot, 0, partner).wait_recv()

    w_all[s] = w_own[...]
    pair_copy.wait()

    def short(stream, two, one, zero):
        w0, w1, w2 = (short_w[j, stream : stream + 1, :] for j in range(3))
        return w0 * zero + w1 * one + w2 * two

    def edge(last, first, streams):
        gives = []
        for stream, before, own in zip(streams, last, first):
            gives.append(
                (
                    short(stream, before[0:1], before[1:2], own[0:1]),
                    short(stream, before[1:2], own[0:1], own[1:2]),
                )
            )
        return gives

    def edge_inner(last, first):
        (k0, k1), (v0, v1) = edge(last, first, (1, 2))
        return rounded(k0 * v0), rounded(k1 * v1)

    own_t, other_t = own_total[...], pair[1, 0:16, :].astype(F32)
    own_edges, other_edges = pair[0, 16:32, :].astype(F32), pair[1, 16:32, :].astype(F32)
    low = k == 0
    t_low, t_high = jnp.where(low, own_t, other_t), jnp.where(low, other_t, own_t)
    e_low, e_high = jnp.where(low, own_edges, other_edges), jnp.where(low, other_edges, own_edges)
    m0, m1 = edge_inner((e_low[4:6], e_low[6:8]), (e_high[0:2], e_high[2:4]))
    chip_total = decay(tokens) * t_low + t_high + scale * (decay(tokens - 1) * m0 + decay(tokens - 2) * m1)
    message = jnp.concatenate([chip_total, e_low[0:4], e_high[4:10], jnp.zeros((6, chans), F32)], axis=0)
    msg[h] = message.astype(BF16)

    def msg_copy(slot, step, chip):
        return pltpu.make_async_remote_copy(
            src_ref=msg.at[slot], dst_ref=msg.at[slot], send_sem=msg_send.at[step], recv_sem=msg_recv.at[slot],
            device_id=(chip * 2 + k, c), device_id_type=MESH,
        )

    def msg_go(step, _):
        msg_copy(h, step, h + step).start()
        return 0

    lax.fori_loop(1, 16 - h, msg_go, 0)

    other_z = 1 - zh
    w_go(s, seq_of(y, other_z, k))
    w_go(s, seq_of(up_y, zh, k))
    w_go(s, seq_of(down_y, zh, k))
    w_go(s, partner)

    far = decay(2 * tokens)
    far1, far2 = scale * decay(2 * tokens - 1), scale * decay(2 * tokens - 2)

    def add_chip(j, carry):
        state, last = carry
        msg_copy(j, 0, h).wait_recv()
        total, edges = msg[j, 0:16, :].astype(F32), msg[j, 16:32, :].astype(F32)
        u0, u1 = edge_inner((last[0:2], last[2:4]), (edges[0:2], edges[2:4]))
        after = jnp.where(j == 0, 0.0, 1.0)
        return far * state + total + after * (far1 * u0 + far2 * u1), edges[4:10]

    chip_in, last = lax.fori_loop(0, h, add_chip, (jnp.zeros((MODES, chans), F32), jnp.zeros((6, chans), F32)))
    f0, f1 = edge_inner((last[0:2], last[2:4]), (e_low[0:2], e_low[2:4]))
    chip_first = jnp.where(h == 0, 0.0, 1.0)
    high_in = decay(tokens) * chip_in + t_low
    high_in += chip_first * scale * (decay(tokens - 1) * f0 + decay(tokens - 2) * f1)
    state_in = jnp.where(low, chip_in, high_in)
    u_first = (jnp.where(low, f0 * chip_first, m0), jnp.where(low, f1 * chip_first, m1))
    first_in = scale * (decay(steps - 1) * u_first[0] + decay(steps - 2) * u_first[1])
    q_last = jnp.where(low, last[4:6], e_low[8:10])
    q_first = edge((q_last,), (ends(0, True),), (0,))[0]

    for tile in range(tiles):
        cut = slice(tile * LANES, tile * LANES + LANES)
        lanes = pl.ds(tile * LANES, LANES)
        skip_row = row(skip, lanes, slice(0, 1))
        state = []
        for m in range(MODES):
            fade = sub_dec[m, :, lanes]
            after = jnp.where(sub1 >= 1, pltpu.roll(fade, 1, 0), 0.0)
            state.append(
                part[m, :, lanes]
                + fade * jnp.broadcast_to(state_in[m : m + 1, cut], (SUBS, LANES))
                + after * jnp.broadcast_to(first_in[m : m + 1, cut], (SUBS, LANES))
            )
        state = tuple(state)

        def gate_step(i, state, first=None, lanes=lanes, tile=tile, cut=cut, skip_row=skip_row):
            state = tuple(row(dec, lanes, 0, slice(m, m + 1)) * state[m] for m in range(MODES))
            conv, q = y_buf[i, :, lanes], q_buf[i, :, lanes]
            if first is not None:
                u = jnp.where(sub1 == 0, jnp.broadcast_to(u_first[first][:, cut], (SUBS, LANES)), 0.0)
                state = tuple(state[m] + row(coef, lanes, slice(m, m + 1)) * u for m in range(MODES))
                conv = conv + skip_row * u
                q = jnp.where(sub1 == 0, jnp.broadcast_to(rounded(q_first[first][:, cut]), (SUBS, LANES)), q)
            conv = rounded(conv + total_of(state))
            g_wide[tile, pl.ds(i, SUBS, stride=steps), :] = q * conv
            return state

        state = gate_step(0, state, 0)
        state = gate_step(1, state, 1)
        lax.fori_loop(2, steps, gate_step, state)
    for tile in range(tiles):
        g_all[c, :, pl.ds(tile * LANES, LANES)] = g_wide[tile].astype(BF16)

    end = (zl == 0) | (zl == 3)
    beside = x * 4 + zl + 1 - 2 * (zl % 2)
    middle = x * 4 + 3 - zl
    order = (zl, zl + 1 - 2 * (zl % 2), 2 - zl // 2, 3 - 3 * (zl // 2))

    def z_copy(slot, at, chan):
        return pltpu.make_async_remote_copy(
            src_ref=g_all.at[slot], dst_ref=g_all.at[slot], send_sem=z_send.at[at], recv_sem=z_recv.at[slot % 4],
            device_id=(s, chan), device_id_type=MESH,
        )

    def x_copy(slot, piece, at, xx):
        rows = pl.ds(piece * half, half)
        return pltpu.make_async_remote_copy(
            src_ref=g_all.at[slot, rows], dst_ref=g_all.at[slot, rows], send_sem=x_send.at[at],
            recv_sem=x_recv.at[slot, piece], device_id=(s, xx * 4 + zl), device_id_type=MESH,
        )

    x_started = []

    def x_go(slot, piece, xx):
        copy = x_copy(slot, piece, len(x_started), xx)
        copy.start()
        x_started.append(copy)

    def own_go(i):
        slot = x * 4 + order[i]
        if i == 0:
            z_copy(slot, 0, beside).start()
            pl.when(jnp.logical_not(end))(lambda: z_copy(slot, 1, middle).start())
        else:
            z_copy(slot, 0, beside).wait_recv()
            onward = middle if i == 1 else beside
            pl.when(jnp.logical_not(end))(lambda: z_copy(slot, 1 + i, onward).start())
        x_go(slot, 0, right)
        x_go(slot, 1, left)
        x_go(slot, 1, right)
        x_go(slot, 0, left)

    def pass_on(i):
        slot = left * 4 + order[i]
        x_copy(slot, 0, 0, right).wait_recv()
        x_go(slot, 0, right)
        slot = right * 4 + order[i]
        x_copy(slot, 1, 0, right).wait_recv()
        x_go(slot, 1, left)

    def multiply(i):
        x_copy(left * 4 + order[i], 1, 0, right).wait_recv()
        x_copy(right * 4 + order[i], 0, 0, right).wait_recv()
        x_copy(across * 4 + order[i], 0, 0, right).wait_recv()
        x_copy(across * 4 + order[i], 1, 0, right).wait_recv()

        def block(xx, _):
            slot = xx * 4 + order[i]
            rows = w_all[pl.ds(2 * slot, 2)].reshape(chans, -1)
            for piece in range(2):
                at = pl.ds(piece * half, half)
                part_sum = jnp.dot(g_all[slot, at], rows, preferred_element_type=F32)
                acc[at] = acc[at] + part_sum
            return 0

        lax.fori_loop(0, 4, block, 0)

    def w_step(n):
        if n == 1:
            slot = seq_of(y, other_z, k)
            w_here(slot)
            w_go(slot, seq_of(up_y, zh, k))
            w_go(slot, seq_of(down_y, zh, k))
            w_go(slot, partner)
        for zz, ups, downs in ((zh, 4, 3), (other_z, 3, 4)):
            for here, limit, onward in (((y + 8 - n) % 8, ups, up_y), ((y + n) % 8, downs, down_y)):
                if n <= limit:
                    slot = seq_of(here, zz, k)
                    w_here(slot)
                    if n < limit:
                        w_go(slot, seq_of(onward, zh, k))
                    w_go(slot, partner)

    acc[...] = jnp.zeros_like(acc)
    own_go(0)
    w_step(1)
    own_go(1)
    pass_on(0)
    w_step(2)
    own_go(2)
    pass_on(1)
    w_step(3)
    own_go(3)
    pass_on(2)
    w_step(4)

    def w_other(at, _):
        w_here(at * 2 + 1 - k)
        return 0

    lax.fori_loop(0, 16, w_other, 0)
    multiply(0)
    multiply(1)
    pass_on(3)
    multiply(2)
    multiply(3)
    out[...] = acc[...].astype(BF16)

    for copy in x_started + w_started:
        copy.wait_send()
    z_copy(c, 0, beside).wait_send()

    @pl.when(jnp.logical_not(end))
    def _():
        for at in range(1, 5):
            z_copy(c, at, beside).wait_send()

    def msg_gone(step, _):
        msg_copy(h, step, h).wait_send()
        return 0

    lax.fori_loop(1, 16 - h, msg_gone, 0)


def body(projected, short_w, residues, rates, skip, w_out):
    tokens, _, chans = projected.shape
    rows, feats = w_out.shape
    length = tokens * lax.axis_size("seq")
    tiles, steps = chans // LANES, tokens // SUBS
    vmem = pl.BlockSpec(memory_space=pltpu.VMEM)
    dma = pltpu.SemaphoreType.DMA
    return pl.pallas_call(
        functools.partial(kernel, length),
        out_shape=jax.ShapeDtypeStruct((tokens, feats), BF16),
        in_specs=[vmem] * 6,
        out_specs=vmem,
        scratch_shapes=[
            pltpu.VMEM((3, tiles, 8 + tokens, LANES), F32),
            pltpu.VMEM((MODES, chans), F32),
            pltpu.VMEM((4, MODES, chans), F32),
            pltpu.VMEM((MODES, SUBS, chans), F32),
            pltpu.VMEM((steps, SUBS, chans), F32),
            pltpu.VMEM((steps, SUBS, chans), F32),
            pltpu.VMEM((steps, SUBS, chans), F32),
            pltpu.VMEM((MODES, SUBS, chans), F32),
            pltpu.VMEM((MODES, chans), F32),
            pltpu.VMEM((2, 32, chans), BF16),
            pltpu.VMEM((16, 32, chans), BF16),
            pltpu.VMEM((tiles, tokens, LANES), F32),
            pltpu.VMEM((16, tokens, chans), BF16),
            pltpu.VMEM((32, rows, feats), BF16),
            pltpu.VMEM((tokens, feats), F32),
            dma((2,)),
            dma((16,)),
            dma((16,)),
            dma((32,)),
            dma((32,)),
            dma((5,)),
            dma((4,)),
            dma((24,)),
            dma((16, 2)),
        ],
        compiler_params=pltpu.CompilerParams(
            collective_id=0, has_side_effects=True, vmem_limit_bytes=48 << 20
        ),
        cost_estimate=pl.CostEstimate(flops=2 * tokens * feats * 4096, bytes_accessed=4 << 20, transcendentals=0),
    )(projected.transpose(1, 0, 2), short_w, residues.T, rates.T, skip.reshape(1, chans), w_out)


def solution(mesh):
    return jax.shard_map(
        body,
        mesh=mesh,
        in_specs=(
            P("seq", None, "chan"),
            P(None, None, "chan"),
            P("chan", None),
            P("chan", None),
            P("chan"),
            P("seq", "chan"),
        ),
        out_specs=P("seq", "chan"),
        check_vma=False,
    )
```

```python
import functools

import jax
import jax.numpy as jnp
from jax import lax
from jax.experimental import pallas as pl
from jax.experimental.pallas import tpu as pltpu
from jax.sharding import PartitionSpec as P

MESH = pl.DeviceIdType.MESH
MODES = 16
SUBS = 8
LANES = 128
PIECES = 4
F32, BF16 = jnp.float32, jnp.bfloat16


def rounded(value):
    return value.astype(BF16).astype(F32)


def total_of(terms):
    terms = list(terms)
    while len(terms) > 1:
        terms = [a + b for a, b in zip(terms[::2], terms[1::2])] + terms[len(terms) // 2 * 2 :]
    return terms[0]


def kernel(
    length,
    proj_hbm,
    short_hbm,
    res_hbm,
    rate_hbm,
    skip_hbm,
    w_hbm,
    out,
    proj,
    short_w,
    res,
    rate,
    skip,
    wide,
    coef,
    dec,
    sub_dec,
    u_buf,
    q_buf,
    y_buf,
    part,
    own_total,
    pair,
    msg,
    edges,
    firsts,
    g_wide,
    g_all,
    w_all,
    acc,
    load_sem,
    pair_sem,
    msg_send,
    msg_recv,
    w_send,
    w_recv,
    z_send,
    z_recv,
    x_send,
    x_recv,
):
    s = lax.axis_index("seq")
    c = lax.axis_index("chan")
    y, zh, k = s // 4, (s // 2) % 2, s % 2
    x, zl = c // 4, c % 4
    h = s // 2
    tokens, chans = proj.shape[1], proj.shape[2]
    tiles = chans // LANES
    steps = tokens // SUBS
    rows_of_piece = tokens // PIECES

    def seq_of(yy, zz, kk):
        return yy * 4 + zz * 2 + kk

    up_y, down_y = (y + 1) % 8, (y + 7) % 8
    right, left, across = (x + 1) % 4, (x + 3) % 4, (x + 2) % 4
    partner = seq_of(y, zh, 1 - k)

    loads = []
    for at, (source, target) in enumerate(
        ((rate_hbm, rate), (res_hbm, res), (short_hbm, short_w), (skip_hbm, skip), (proj_hbm, proj), (w_hbm, w_all.at[s]))
    ):
        loads.append(pltpu.make_async_copy(source, target, load_sem.at[at]))
        loads[-1].start()

    barrier = pltpu.get_barrier_semaphore()

    def greet(seq, chan):
        pl.semaphore_signal(barrier, inc=1, device_id=(seq, chan), device_id_type=MESH)

    greet(partner, c)
    for step in (1, 3):
        greet(s, (x + step) % 4 * 4 + zl)
        greet(s, x * 4 + (zl + step) % 4)

    def greet_chip(step, _):
        greet((h + step) % 16 * 2 + k, c)
        return 0

    lax.fori_loop(1, 16, greet_chip, 0)

    acc[...] = jnp.zeros_like(acc)
    edges[...] = jnp.zeros_like(edges)

    for copy in loads[:4]:
        copy.wait()
    speed = rate[...] * (1.0 / length)
    scale = res[...] * jnp.sqrt(2.0 * rate[...] * (1.0 / length))
    coef[...] = scale

    def decay(count):
        return jnp.exp(speed * (-1.0 * count))

    for at, count in enumerate((1, steps, 2 * steps, 4 * steps)):
        dec[at] = decay(count)
    sub = lax.broadcasted_iota(jnp.int32, (SUBS, chans), 0)
    sub_steps = sub.astype(F32) * (-1.0 * steps)
    for m in range(MODES):
        sub_dec[m] = jnp.exp(jnp.broadcast_to(speed[m : m + 1], (SUBS, chans)) * sub_steps)

    loads[4].wait()
    for stream in range(3):
        for tile in range(tiles):
            lanes = pl.ds(tile * LANES, LANES)
            wide[stream, tile, 0:8, :] = jnp.zeros((8, LANES), F32)
            wide[stream, tile, 8 : 8 + tokens, :] = proj[stream, :, lanes].astype(F32)

    sub1 = lax.broadcasted_iota(jnp.int32, (SUBS, LANES), 0)
    keep = jnp.where((sub1 > 0) | (s == 0), 1.0, 0.0).astype(F32)

    def row(ref, lanes, *index):
        return jnp.broadcast_to(ref[index + (lanes,)], (SUBS, LANES))

    for tile in range(tiles):
        lanes = pl.ds(tile * LANES, LANES)
        taps = [[row(short_w, lanes, j, slice(st, st + 1)) for j in range(3)] for st in range(3)]
        skip_row = row(skip, lanes, slice(0, 1))

        def rows_at(stream, start, tile=tile):
            return wide[stream, tile, pl.ds(start, SUBS, stride=steps), :]

        def scan_step(i, carry, first=False, tile=tile, lanes=lanes, taps=taps, skip_row=skip_row):
            state, behind = carry
            feats, now = [], []
            for st in range(3):
                value = rows_at(st, 8 + i)
                one, two = behind[st]
                feats.append(taps[st][0] * value + taps[st][1] * one + taps[st][2] * two)
                now.append((value, one))
            u = rounded(feats[1] * feats[2])
            if first:
                u = u * keep
            state = tuple(
                row(dec, lanes, 0, slice(m, m + 1)) * state[m] + row(coef, lanes, slice(m, m + 1)) * u
                for m in range(MODES)
            )
            q_buf[i, :, lanes] = rounded(feats[0])
            u_buf[i, :, lanes] = u
            y_buf[i, :, lanes] = total_of(state) + skip_row * u
            return state, tuple(now)

        carry = (
            tuple(jnp.zeros((SUBS, LANES), F32) for _ in range(MODES)),
            tuple((rows_at(st, 7), rows_at(st, 6)) for st in range(3)),
        )
        carry = scan_step(0, carry, True)
        carry = scan_step(1, carry, True)
        state, _ = lax.fori_loop(2, steps, scan_step, carry)
        for m in range(MODES):
            value = state[m]
            for at, shift in ((1, 1), (2, 2), (3, 4)):
                moved = pltpu.roll(value, shift, 0)
                value = value + row(dec, lanes, at, slice(m, m + 1)) * jnp.where(sub1 >= shift, moved, 0.0)
            own_total[m : m + 1, lanes] = value[SUBS - 1 : SUBS]
            part[m, :, lanes] = jnp.where(sub1 >= 1, pltpu.roll(value, 1, 0), 0.0)

    def ends(stream, first):
        start = 0 if first else tokens - 2
        return jnp.concatenate([wide[stream, t, pl.ds(8 + start, 2), :] for t in range(tiles)], axis=1)

    mine = [own_total[...]]
    mine += [ends(1, True), ends(2, True), ends(1, False), ends(2, False), ends(0, False)]
    mine += [jnp.zeros((6, chans), F32)]
    pair[0] = jnp.concatenate(mine, axis=0).astype(BF16)

    pl.semaphore_wait(barrier, 20)

    pair_copy = pltpu.make_async_remote_copy(
        src_ref=pair.at[0], dst_ref=pair.at[1], send_sem=pair_sem.at[0], recv_sem=pair_sem.at[1],
        device_id=(partner, c), device_id_type=MESH,
    )
    pair_copy.start()

    def w_copy(slot, at, seq):
        return pltpu.make_async_remote_copy(
            src_ref=w_all.at[slot], dst_ref=w_all.at[slot], send_sem=w_send.at[at], recv_sem=w_recv.at[slot],
            device_id=(seq, c), device_id_type=MESH,
        )

    w_started = []

    def w_go(slot, seq):
        copy = w_copy(slot, len(w_started), seq)
        copy.start()
        w_started.append(copy)

    def w_here(slot):
        w_copy(slot, 0, partner).wait_recv()

    pair_copy.wait()

    def short(stream, two, one, zero):
        w0, w1, w2 = (short_w[j, stream : stream + 1, :] for j in range(3))
        return w0 * zero + w1 * one + w2 * two

    def edge(last, first, streams):
        gives = []
        for stream, before, own in zip(streams, last, first):
            gives.append(
                (
                    short(stream, before[0:1], before[1:2], own[0:1]),
                    short(stream, before[1:2], own[0:1], own[1:2]),
                )
            )
        return gives

    def edge_inner(last, first):
        (k0, k1), (v0, v1) = edge(last, first, (1, 2))
        return rounded(k0 * v0), rounded(k1 * v1)

    own_t, other_t = own_total[...], pair[1, 0:16, :].astype(F32)
    own_edges, other_edges = pair[0, 16:32, :].astype(F32), pair[1, 16:32, :].astype(F32)
    low = k == 0
    t_low, t_high = jnp.where(low, own_t, other_t), jnp.where(low, other_t, own_t)
    e_low, e_high = jnp.where(low, own_edges, other_edges), jnp.where(low, other_edges, own_edges)
    m0, m1 = edge_inner((e_low[4:6], e_low[6:8]), (e_high[0:2], e_high[2:4]))
    chip_total = decay(tokens) * t_low + t_high + scale * (decay(tokens - 1) * m0 + decay(tokens - 2) * m1)
    message = jnp.concatenate([chip_total, e_low[0:4], e_high[4:10], jnp.zeros((6, chans), F32)], axis=0)
    msg[h] = message.astype(BF16)

    def msg_copy(slot, step, chip):
        return pltpu.make_async_remote_copy(
            src_ref=msg.at[slot], dst_ref=msg.at[slot], send_sem=msg_send.at[step], recv_sem=msg_recv.at[slot],
            device_id=(chip * 2 + k, c), device_id_type=MESH,
        )

    def msg_go(step, _):
        msg_copy(h, step, h + step).start()
        return 0

    lax.fori_loop(1, 16 - h, msg_go, 0)

    loads[5].wait()
    other_z = 1 - zh
    w_go(s, seq_of(y, other_z, k))
    w_go(s, seq_of(up_y, zh, k))
    w_go(s, seq_of(down_y, zh, k))
    w_go(s, partner)

    far = decay(2 * tokens)
    far1, far2 = scale * decay(2 * tokens - 1), scale * decay(2 * tokens - 2)

    def put_edges(j):
        values = msg[j, 16:32, :].astype(F32)
        for tile in range(tiles):
            edges[tile, pl.ds(j * 16 + 16, 16), :] = values[:, tile * LANES : tile * LANES + LANES]

    def chip_here(j, _):
        msg_copy(j, 0, h).wait_recv()
        put_edges(j)
        return 0

    put_edges(h)
    lax.fori_loop(0, h, chip_here, 0)
    for tile in range(tiles):
        lanes = pl.ds(tile * LANES, LANES)

        def taps_of(stream, lanes=lanes):
            return [jnp.broadcast_to(short_w[j, stream : stream + 1, lanes], (16, LANES)) for j in range(3)]

        def edge_rows(at, before, tile=tile):
            return edges[tile, pl.ds(at + (0 if before else 16), 16, stride=16), :]

        (k0, k1), (v0, v1) = (
            (
                w0 * edge_rows(2 * st, False) + w1 * edge_rows(5 + 2 * st, True) + w2 * edge_rows(4 + 2 * st, True),
                w0 * edge_rows(2 * st + 1, False) + w1 * edge_rows(2 * st, False) + w2 * edge_rows(5 + 2 * st, True),
            )
            for st, (w0, w1, w2) in enumerate((taps_of(1), taps_of(2)))
        )
        firsts[0, :, lanes] = rounded(k0 * v0)
        firsts[1, :, lanes] = rounded(k1 * v1)

    def add_chip(j, state):
        after = jnp.where(j == 0, 0.0, 1.0)
        u0, u1 = firsts[0, pl.ds(j, 1), :], firsts[1, pl.ds(j, 1), :]
        return far * state + msg[j, 0:16, :].astype(F32) + after * (far1 * u0 + far2 * u1)

    chip_in = lax.fori_loop(0, h, add_chip, jnp.zeros((MODES, chans), F32))
    f0, f1 = firsts[0, pl.ds(h, 1), :], firsts[1, pl.ds(h, 1), :]
    chip_first = jnp.where(h == 0, 0.0, 1.0)
    chip_last_q = jnp.concatenate([edges[tile, pl.ds(h * 16 + 8, 2), :] for tile in range(tiles)], axis=1)
    high_in = decay(tokens) * chip_in + t_low
    high_in += chip_first * scale * (decay(tokens - 1) * f0 + decay(tokens - 2) * f1)
    state_in = jnp.where(low, chip_in, high_in)
    u_first = (jnp.where(low, f0 * chip_first, m0), jnp.where(low, f1 * chip_first, m1))
    first_in = scale * (decay(steps - 1) * u_first[0] + decay(steps - 2) * u_first[1])
    q_last = jnp.where(low, chip_last_q, e_low[8:10])
    q_first = edge((q_last,), (ends(0, True),), (0,))[0]

    for tile in range(tiles):
        cut = slice(tile * LANES, tile * LANES + LANES)
        lanes = pl.ds(tile * LANES, LANES)
        skip_row = row(skip, lanes, slice(0, 1))
        state = []
        for m in range(MODES):
            fade = sub_dec[m, :, lanes]
            after = jnp.where(sub1 >= 1, pltpu.roll(fade, 1, 0), 0.0)
            state.append(
                part[m, :, lanes]
                + fade * jnp.broadcast_to(state_in[m : m + 1, cut], (SUBS, LANES))
                + after * jnp.broadcast_to(first_in[m : m + 1, cut], (SUBS, LANES))
            )
        state = tuple(state)

        def gate_step(i, state, first=None, lanes=lanes, tile=tile, cut=cut, skip_row=skip_row):
            state = tuple(row(dec, lanes, 0, slice(m, m + 1)) * state[m] for m in range(MODES))
            conv, q = y_buf[i, :, lanes], q_buf[i, :, lanes]
            if first is not None:
                u = jnp.where(sub1 == 0, jnp.broadcast_to(u_first[first][:, cut], (SUBS, LANES)), 0.0)
                state = tuple(state[m] + row(coef, lanes, slice(m, m + 1)) * u for m in range(MODES))
                conv = conv + skip_row * u
                q = jnp.where(sub1 == 0, jnp.broadcast_to(rounded(q_first[first][:, cut]), (SUBS, LANES)), q)
            conv = rounded(conv + total_of(state))
            g_wide[tile, pl.ds(i, SUBS, stride=steps), :] = q * conv
            return state

        state = gate_step(0, state, 0)
        state = gate_step(1, state, 1)
        lax.fori_loop(2, steps, gate_step, state)
    for tile in range(tiles):
        g_all[c, :, pl.ds(tile * LANES, LANES)] = g_wide[tile].astype(BF16)

    end = (zl == 0) | (zl == 3)
    beside = x * 4 + zl + 1 - 2 * (zl % 2)
    middle = x * 4 + 3 - zl
    order = (zl, zl + 1 - 2 * (zl % 2), 2 - zl // 2, 3 - 3 * (zl // 2))

    def z_copy(slot, piece, at, chan):
        rows = pl.ds(piece * rows_of_piece, rows_of_piece)
        return pltpu.make_async_remote_copy(
            src_ref=g_all.at[slot, rows], dst_ref=g_all.at[slot, rows], send_sem=z_send.at[at, piece],
            recv_sem=z_recv.at[slot % 4, piece], device_id=(s, chan), device_id_type=MESH,
        )

    def x_copy(slot, piece, at, xx):
        rows = pl.ds(piece * rows_of_piece, rows_of_piece)
        return pltpu.make_async_remote_copy(
            src_ref=g_all.at[slot, rows], dst_ref=g_all.at[slot, rows], send_sem=x_send.at[at],
            recv_sem=x_recv.at[slot, piece], device_id=(s, xx * 4 + zl), device_id_type=MESH,
        )

    x_started = []

    def x_go(slot, piece, xx):
        copy = x_copy(slot, piece, len(x_started), xx)
        copy.start()
        x_started.append(copy)

    def x_here(slot, piece):
        x_copy(slot, piece, 0, right).wait_recv()

    def own_go():
        for piece in range(PIECES):
            z_copy(c, piece, 0, beside).start()
            x_go(c, piece, right)
            pl.when(jnp.logical_not(end))(lambda piece=piece: z_copy(c, piece, 1, middle).start())
            x_go(c, (piece + PIECES // 2) % PIECES, left)

    def along(i, piece):
        slot = x * 4 + order[i]
        z_copy(slot, piece, 0, beside).wait_recv()
        onward = middle if i == 1 else beside
        pl.when(jnp.logical_not(end))(lambda: z_copy(slot, piece, 1 + i, onward).start())
        x_go(slot, piece, right)
        x_go(slot, piece, left)

    def pass_on(i, piece):
        if piece < PIECES // 2:
            slot, onward = left * 4 + order[i], right
        else:
            slot, onward = right * 4 + order[i], left
        x_here(slot, piece)
        x_go(slot, piece, onward)

    place = dict(own=x, left=left, right=right, across=across)

    def multiply(i, sides):
        for piece in range(PIECES):
            if 'left' in sides and piece >= PIECES // 2:
                x_here(left * 4 + order[i], piece)
            if 'right' in sides and piece < PIECES // 2:
                x_here(right * 4 + order[i], piece)
            if 'across' in sides:
                x_here(across * 4 + order[i], piece)

        def block(at, _):
            at = pl.ds(pl.multiple_of(at * 256, 256), 256)
            value = acc[at]
            for side in sides:
                slot = place[side] * 4 + order[i]
                rows = w_all[pl.ds(2 * slot, 2)].reshape(chans, -1)
                value = value + jnp.dot(g_all[slot, at], rows, preferred_element_type=F32)
            acc[at] = value
            return 0

        lax.fori_loop(0, tokens // 256, block, 0)

    def w_step(n):
        if n == 1:
            slot = seq_of(y, other_z, k)
            w_here(slot)
            w_go(slot, seq_of(up_y, zh, k))
            w_go(slot, seq_of(down_y, zh, k))
            w_go(slot, partner)
        for zz, ups, downs in ((zh, 4, 3), (other_z, 3, 4)):
            for here, limit, onward in (((y + 8 - n) % 8, ups, up_y), ((y + n) % 8, downs, down_y)):
                if n <= limit:
                    slot = seq_of(here, zz, k)
                    w_here(slot)
                    if n < limit:
                        w_go(slot, seq_of(onward, zh, k))
                    w_go(slot, partner)

    def w_other(at, _):
        w_here(at * 2 + 1 - k)
        return 0

    own_go()
    w_step(1)
    along(1, 0)
    along(1, 1)
    pass_on(0, 0)
    pass_on(0, 2)
    along(2, 0)
    pass_on(0, 1)
    pass_on(0, 3)
    along(1, 2)
    along(2, 1)
    along(1, 3)
    along(2, 2)
    along(2, 3)
    w_step(2)
    for piece in range(PIECES):
        along(3, piece)
    for piece in (0, 2, 1, 3):
        pass_on(1, piece)
    w_step(3)
    for piece in (0, 2, 1, 3):
        pass_on(2, piece)
    w_step(4)
    lax.fori_loop(0, 16, w_other, 0)
    everyone = tuple(place)
    multiply(0, everyone)
    multiply(1, everyone)
    for piece in (0, 2, 1, 3):
        pass_on(3, piece)
    multiply(2, everyone)
    multiply(3, ('own', 'left', 'right'))
    multiply(3, ('across',))
    out[...] = acc[...].astype(BF16)

    for copy in x_started + w_started:
        copy.wait_send()
    for piece in range(PIECES):
        z_copy(c, piece, 0, beside).wait_send()

    @pl.when(jnp.logical_not(end))
    def _():
        for at in range(1, 5):
            for piece in range(PIECES):
                z_copy(c, piece, at, beside).wait_send()

    def msg_gone(step, _):
        msg_copy(h, step, h).wait_send()
        return 0

    lax.fori_loop(1, 16 - h, msg_gone, 0)


def body(projected, short_w, residues, rates, skip, w_out):
    tokens, _, chans = projected.shape
    rows, feats = w_out.shape
    length = tokens * lax.axis_size("seq")
    tiles, steps = chans // LANES, tokens // SUBS
    vmem = pl.BlockSpec(memory_space=pltpu.VMEM)
    dma = pltpu.SemaphoreType.DMA
    return pl.pallas_call(
        functools.partial(kernel, length),
        out_shape=jax.ShapeDtypeStruct((tokens, feats), BF16),
        in_specs=[pl.BlockSpec(memory_space=pltpu.HBM)] * 6,
        out_specs=vmem,
        scratch_shapes=[
            pltpu.VMEM((3, tokens, chans), BF16),
            pltpu.VMEM((3, 3, chans), F32),
            pltpu.VMEM((MODES, chans), F32),
            pltpu.VMEM((MODES, chans), F32),
            pltpu.VMEM((1, chans), F32),
            pltpu.VMEM((3, tiles, 8 + tokens, LANES), F32),
            pltpu.VMEM((MODES, chans), F32),
            pltpu.VMEM((4, MODES, chans), F32),
            pltpu.VMEM((MODES, SUBS, chans), F32),
            pltpu.VMEM((steps, SUBS, chans), F32),
            pltpu.VMEM((steps, SUBS, chans), F32),
            pltpu.VMEM((steps, SUBS, chans), F32),
            pltpu.VMEM((MODES, SUBS, chans), F32),
            pltpu.VMEM((MODES, chans), F32),
            pltpu.VMEM((2, 32, chans), BF16),
            pltpu.VMEM((16, 32, chans), BF16),
            pltpu.VMEM((tiles, 17 * 16, LANES), F32),
            pltpu.VMEM((2, 16, chans), F32),
            pltpu.VMEM((tiles, tokens, LANES), F32),
            pltpu.VMEM((16, tokens, chans), BF16),
            pltpu.VMEM((32, rows, feats), BF16),
            pltpu.VMEM((tokens, feats), F32),
            dma((6,)),
            dma((2,)),
            dma((16,)),
            dma((16,)),
            dma((32,)),
            dma((32,)),
            dma((5, PIECES)),
            dma((4, PIECES)),
            dma((12 * PIECES,)),
            dma((16, PIECES)),
        ],
        compiler_params=pltpu.CompilerParams(
            collective_id=0, has_side_effects=True, vmem_limit_bytes=63 << 20
        ),
        cost_estimate=pl.CostEstimate(flops=2 * tokens * feats * 4096, bytes_accessed=4 << 20, transcendentals=0),
    )(projected.transpose(1, 0, 2), short_w, residues.T, rates.T, skip.reshape(1, chans), w_out)


def solution(mesh):
    return jax.shard_map(
        body,
        mesh=mesh,
        in_specs=(
            P("seq", None, "chan"),
            P(None, None, "chan"),
            P("chan", None),
            P("chan", None),
            P("chan"),
            P("seq", "chan"),
        ),
        out_specs=P("seq", "chan"),
        check_vma=False,
    )
```

```python
import functools

import jax
import jax.numpy as jnp
from jax import lax
from jax.experimental import pallas as pl
from jax.experimental.pallas import tpu as pltpu
from jax.sharding import PartitionSpec as P

MESH = pl.DeviceIdType.MESH
MODES = 16
SUBS = 8
LANES = 128
PIECES = 4
F32, BF16 = jnp.float32, jnp.bfloat16


def rounded(value):
    return value.astype(BF16).astype(F32)


def total_of(terms):
    terms = list(terms)
    while len(terms) > 1:
        terms = [a + b for a, b in zip(terms[::2], terms[1::2])] + terms[len(terms) // 2 * 2 :]
    return terms[0]


def kernel(
    length,
    proj_hbm,
    short_hbm,
    res_hbm,
    rate_hbm,
    skip_hbm,
    w_hbm,
    out,
    proj,
    short_w,
    res,
    rate,
    skip,
    wide,
    coef,
    dec,
    sub_dec,
    u_buf,
    q_buf,
    y_buf,
    part,
    own_total,
    pair,
    msg,
    edges,
    firsts,
    g_wide,
    g_all,
    w_all,
    acc,
    load_sem,
    pair_sem,
    msg_send,
    msg_recv,
    w_send,
    w_recv,
    z_send,
    z_recv,
    x_send,
    x_recv,
):
    s = lax.axis_index("seq")
    c = lax.axis_index("chan")
    y, zh, k = s // 4, (s // 2) % 2, s % 2
    x, zl = c // 4, c % 4
    h = s // 2
    tokens, chans = proj.shape[1], proj.shape[2]
    tiles = chans // LANES
    steps = tokens // SUBS
    rows_of_piece = tokens // PIECES

    def seq_of(yy, zz, kk):
        return yy * 4 + zz * 2 + kk

    up_y, down_y = (y + 1) % 8, (y + 7) % 8
    right, left, across = (x + 1) % 4, (x + 3) % 4, (x + 2) % 4
    partner = seq_of(y, zh, 1 - k)

    loads = []
    for at, (source, target) in enumerate(
        ((rate_hbm, rate), (res_hbm, res), (short_hbm, short_w), (skip_hbm, skip), (proj_hbm, proj), (w_hbm, w_all.at[s]))
    ):
        loads.append(pltpu.make_async_copy(source, target, load_sem.at[at]))
        loads[-1].start()

    barrier = pltpu.get_barrier_semaphore()

    def greet(seq, chan):
        pl.semaphore_signal(barrier, inc=1, device_id=(seq, chan), device_id_type=MESH)

    greet(partner, c)
    for step in (1, 3):
        greet(s, (x + step) % 4 * 4 + zl)
        greet(s, x * 4 + (zl + step) % 4)

    def greet_chip(step, _):
        greet((h + step) % 16 * 2 + k, c)
        return 0

    lax.fori_loop(1, 16, greet_chip, 0)

    acc[...] = jnp.zeros_like(acc)
    edges[...] = jnp.zeros_like(edges)

    for copy in loads[:4]:
        copy.wait()
    speed = rate[...] * (1.0 / length)
    scale = res[...] * jnp.sqrt(2.0 * rate[...] * (1.0 / length))
    coef[...] = scale

    def decay(count):
        return jnp.exp(speed * (-1.0 * count))

    for at, count in enumerate((1, steps, 2 * steps, 4 * steps)):
        dec[at] = decay(count)
    sub = lax.broadcasted_iota(jnp.int32, (SUBS, chans), 0)
    sub_steps = sub.astype(F32) * (-1.0 * steps)
    for m in range(MODES):
        sub_dec[m] = jnp.exp(jnp.broadcast_to(speed[m : m + 1], (SUBS, chans)) * sub_steps)

    loads[4].wait()
    for stream in range(3):
        for tile in range(tiles):
            lanes = pl.ds(tile * LANES, LANES)
            wide[stream, tile, 0:8, :] = jnp.zeros((8, LANES), F32)
            wide[stream, tile, 8 : 8 + tokens, :] = proj[stream, :, lanes].astype(F32)

    sub1 = lax.broadcasted_iota(jnp.int32, (SUBS, LANES), 0)
    keep = jnp.where((sub1 > 0) | (s == 0), 1.0, 0.0).astype(F32)

    def row(ref, lanes, *index):
        return jnp.broadcast_to(ref[index + (lanes,)], (SUBS, LANES))

    for tile in range(tiles):
        lanes = pl.ds(tile * LANES, LANES)
        taps = [[row(short_w, lanes, j, slice(st, st + 1)) for j in range(3)] for st in range(3)]
        skip_row = row(skip, lanes, slice(0, 1))

        def rows_at(stream, start, tile=tile):
            return wide[stream, tile, pl.ds(start, SUBS, stride=steps), :]

        def scan_step(i, carry, first=False, tile=tile, lanes=lanes, taps=taps, skip_row=skip_row):
            state, behind = carry
            feats, now = [], []
            for st in range(3):
                value = rows_at(st, 8 + i)
                one, two = behind[st]
                feats.append(taps[st][0] * value + taps[st][1] * one + taps[st][2] * two)
                now.append((value, one))
            u = rounded(feats[1] * feats[2])
            if first:
                u = u * keep
            state = tuple(
                row(dec, lanes, 0, slice(m, m + 1)) * state[m] + row(coef, lanes, slice(m, m + 1)) * u
                for m in range(MODES)
            )
            q_buf[i, :, lanes] = rounded(feats[0])
            u_buf[i, :, lanes] = u
            y_buf[i, :, lanes] = total_of(state) + skip_row * u
            return state, tuple(now)

        carry = (
            tuple(jnp.zeros((SUBS, LANES), F32) for _ in range(MODES)),
            tuple((rows_at(st, 7), rows_at(st, 6)) for st in range(3)),
        )
        carry = scan_step(0, carry, True)
        carry = scan_step(1, carry, True)
        state, _ = lax.fori_loop(2, steps, scan_step, carry)
        for m in range(MODES):
            value = state[m]
            for at, shift in ((1, 1), (2, 2), (3, 4)):
                moved = pltpu.roll(value, shift, 0)
                value = value + row(dec, lanes, at, slice(m, m + 1)) * jnp.where(sub1 >= shift, moved, 0.0)
            own_total[m : m + 1, lanes] = value[SUBS - 1 : SUBS]
            part[m, :, lanes] = jnp.where(sub1 >= 1, pltpu.roll(value, 1, 0), 0.0)

    def ends(stream, first):
        start = 0 if first else tokens - 2
        return jnp.concatenate([wide[stream, t, pl.ds(8 + start, 2), :] for t in range(tiles)], axis=1)

    mine = [own_total[...]]
    mine += [ends(1, True), ends(2, True), ends(1, False), ends(2, False), ends(0, False)]
    mine += [jnp.zeros((6, chans), F32)]
    pair[0] = jnp.concatenate(mine, axis=0).astype(BF16)

    pl.semaphore_wait(barrier, 20)

    pair_copy = pltpu.make_async_remote_copy(
        src_ref=pair.at[0], dst_ref=pair.at[1], send_sem=pair_sem.at[0], recv_sem=pair_sem.at[1],
        device_id=(partner, c), device_id_type=MESH,
    )
    pair_copy.start()

    def w_copy(slot, at, seq):
        return pltpu.make_async_remote_copy(
            src_ref=w_all.at[slot], dst_ref=w_all.at[slot], send_sem=w_send.at[at], recv_sem=w_recv.at[slot],
            device_id=(seq, c), device_id_type=MESH,
        )

    w_started = []

    def w_go(slot, seq):
        copy = w_copy(slot, len(w_started), seq)
        copy.start()
        w_started.append(copy)

    def w_here(slot):
        w_copy(slot, 0, partner).wait_recv()

    pair_copy.wait()

    def short(stream, two, one, zero):
        w0, w1, w2 = (short_w[j, stream : stream + 1, :] for j in range(3))
        return w0 * zero + w1 * one + w2 * two

    def edge(last, first, streams):
        gives = []
        for stream, before, own in zip(streams, last, first):
            gives.append(
                (
                    short(stream, before[0:1], before[1:2], own[0:1]),
                    short(stream, before[1:2], own[0:1], own[1:2]),
                )
            )
        return gives

    def edge_inner(last, first):
        (k0, k1), (v0, v1) = edge(last, first, (1, 2))
        return rounded(k0 * v0), rounded(k1 * v1)

    own_t, other_t = own_total[...], pair[1, 0:16, :].astype(F32)
    own_edges, other_edges = pair[0, 16:32, :].astype(F32), pair[1, 16:32, :].astype(F32)
    low = k == 0
    t_low, t_high = jnp.where(low, own_t, other_t), jnp.where(low, other_t, own_t)
    e_low, e_high = jnp.where(low, own_edges, other_edges), jnp.where(low, other_edges, own_edges)
    m0, m1 = edge_inner((e_low[4:6], e_low[6:8]), (e_high[0:2], e_high[2:4]))
    chip_total = decay(tokens) * t_low + t_high + scale * (decay(tokens - 1) * m0 + decay(tokens - 2) * m1)
    for at, parts in enumerate(
        (
            (chip_total[0:8], e_low[0:4], jnp.zeros((4, chans), F32)),
            (chip_total[8:16], e_high[4:10], jnp.zeros((2, chans), F32)),
        )
    ):
        msg[h, at] = jnp.concatenate(parts, axis=0).astype(BF16)

    def msg_copy(slot, part_at, step, seq):
        return pltpu.make_async_remote_copy(
            src_ref=msg.at[slot, part_at], dst_ref=msg.at[slot, part_at], send_sem=msg_send.at[step],
            recv_sem=msg_recv.at[slot, part_at], device_id=(seq, c), device_id_type=MESH,
        )

    def msg_go(step, _):
        msg_copy(h, k, step, (h + step) * 2 + k).start()
        return 0

    lax.fori_loop(1, 16 - h, msg_go, 0)

    def w_chain(own, n):
        zz, ups, downs = (zh, 4, 3) if own else (other_z, 3, 4)
        if n == 0:
            slot = seq_of(y, zz, k)
            w_here(slot)
            w_go(slot, seq_of(up_y, zh, k))
            w_go(slot, seq_of(down_y, zh, k))
            w_go(slot, partner)
            return
        for here, limit, onward in (((y + 8 - n) % 8, ups, up_y), ((y + n) % 8, downs, down_y)):
            if n <= limit:
                slot = seq_of(here, zz, k)
                w_here(slot)
                if n < limit:
                    w_go(slot, seq_of(onward, zh, k))
                w_go(slot, partner)

    loads[5].wait()
    other_z = 1 - zh
    w_go(s, seq_of(y, other_z, k))
    w_go(s, seq_of(up_y, zh, k))
    w_go(s, seq_of(down_y, zh, k))
    w_go(s, partner)

    far = decay(2 * tokens)
    far1, far2 = scale * decay(2 * tokens - 1), scale * decay(2 * tokens - 2)

    def put_edges(j):
        for at in range(2):
            values = msg[j, at].astype(F32)[8:16]
            for tile in range(tiles):
                edges[tile, pl.ds(j * 16 + 16 + 8 * at, 8), :] = values[:, tile * LANES : tile * LANES + LANES]

    def half_here(j, _):
        msg_copy(j, k, 0, s).wait_recv()
        msg_copy(j, k, 16 + j, partner).start()
        return 0

    def chip_here(j, _):
        msg_copy(j, 1 - k, 0, s).wait_recv()
        put_edges(j)
        return 0

    put_edges(h)
    w_chain(True, 1)
    lax.fori_loop(0, h, half_here, 0)
    w_chain(False, 0)
    lax.fori_loop(0, h, chip_here, 0)
    for tile in range(tiles):
        lanes = pl.ds(tile * LANES, LANES)

        def taps_of(stream, lanes=lanes):
            return [jnp.broadcast_to(short_w[j, stream : stream + 1, lanes], (16, LANES)) for j in range(3)]

        def edge_rows(at, before, tile=tile):
            return edges[tile, pl.ds(at + (0 if before else 16), 16, stride=16), :]

        (k0, k1), (v0, v1) = (
            (
                w0 * edge_rows(2 * st, False) + w1 * edge_rows(9 + 2 * st, True) + w2 * edge_rows(8 + 2 * st, True),
                w0 * edge_rows(2 * st + 1, False) + w1 * edge_rows(2 * st, False) + w2 * edge_rows(9 + 2 * st, True),
            )
            for st, (w0, w1, w2) in enumerate((taps_of(1), taps_of(2)))
        )
        firsts[0, :, lanes] = rounded(k0 * v0)
        firsts[1, :, lanes] = rounded(k1 * v1)

    def add_chip(j, state):
        after = jnp.where(j == 0, 0.0, 1.0)
        u0, u1 = firsts[0, pl.ds(j, 1), :], firsts[1, pl.ds(j, 1), :]
        total = jnp.concatenate([msg[j, at].astype(F32)[0:8] for at in range(2)], axis=0)
        return far * state + total + after * (far1 * u0 + far2 * u1)

    chip_in = lax.fori_loop(0, h, add_chip, jnp.zeros((MODES, chans), F32))
    f0, f1 = firsts[0, pl.ds(h, 1), :], firsts[1, pl.ds(h, 1), :]
    chip_first = jnp.where(h == 0, 0.0, 1.0)
    chip_last_q = jnp.concatenate([edges[tile, pl.ds(h * 16 + 12, 2), :] for tile in range(tiles)], axis=1)
    high_in = decay(tokens) * chip_in + t_low
    high_in += chip_first * scale * (decay(tokens - 1) * f0 + decay(tokens - 2) * f1)
    state_in = jnp.where(low, chip_in, high_in)
    u_first = (jnp.where(low, f0 * chip_first, m0), jnp.where(low, f1 * chip_first, m1))
    first_in = scale * (decay(steps - 1) * u_first[0] + decay(steps - 2) * u_first[1])
    q_last = jnp.where(low, chip_last_q, e_low[8:10])
    q_first = edge((q_last,), (ends(0, True),), (0,))[0]

    for tile in range(tiles):
        cut = slice(tile * LANES, tile * LANES + LANES)
        lanes = pl.ds(tile * LANES, LANES)
        skip_row = row(skip, lanes, slice(0, 1))
        state = []
        for m in range(MODES):
            fade = sub_dec[m, :, lanes]
            after = jnp.where(sub1 >= 1, pltpu.roll(fade, 1, 0), 0.0)
            state.append(
                part[m, :, lanes]
                + fade * jnp.broadcast_to(state_in[m : m + 1, cut], (SUBS, LANES))
                + after * jnp.broadcast_to(first_in[m : m + 1, cut], (SUBS, LANES))
            )
        state = tuple(state)

        def gate_step(i, state, first=None, lanes=lanes, tile=tile, cut=cut, skip_row=skip_row):
            state = tuple(row(dec, lanes, 0, slice(m, m + 1)) * state[m] for m in range(MODES))
            conv, q = y_buf[i, :, lanes], q_buf[i, :, lanes]
            if first is not None:
                u = jnp.where(sub1 == 0, jnp.broadcast_to(u_first[first][:, cut], (SUBS, LANES)), 0.0)
                state = tuple(state[m] + row(coef, lanes, slice(m, m + 1)) * u for m in range(MODES))
                conv = conv + skip_row * u
                q = jnp.where(sub1 == 0, jnp.broadcast_to(rounded(q_first[first][:, cut]), (SUBS, LANES)), q)
            conv = rounded(conv + total_of(state))
            g_wide[tile, pl.ds(i, SUBS, stride=steps), :] = q * conv
            return state

        state = gate_step(0, state, 0)
        state = gate_step(1, state, 1)
        lax.fori_loop(2, steps, gate_step, state)
    for tile in range(tiles):
        g_all[c, :, pl.ds(tile * LANES, LANES)] = g_wide[tile].astype(BF16)

    end = (zl == 0) | (zl == 3)
    beside = x * 4 + zl + 1 - 2 * (zl % 2)
    middle = x * 4 + 3 - zl
    order = (zl, zl + 1 - 2 * (zl % 2), 2 - zl // 2, 3 - 3 * (zl // 2))

    def z_copy(slot, piece, at, chan):
        rows = pl.ds(piece * rows_of_piece, rows_of_piece)
        return pltpu.make_async_remote_copy(
            src_ref=g_all.at[slot, rows], dst_ref=g_all.at[slot, rows], send_sem=z_send.at[at, piece],
            recv_sem=z_recv.at[slot % 4, piece], device_id=(s, chan), device_id_type=MESH,
        )

    def x_copy(slot, piece, at, xx):
        rows = pl.ds(piece * rows_of_piece, rows_of_piece)
        return pltpu.make_async_remote_copy(
            src_ref=g_all.at[slot, rows], dst_ref=g_all.at[slot, rows], send_sem=x_send.at[at],
            recv_sem=x_recv.at[slot, piece], device_id=(s, xx * 4 + zl), device_id_type=MESH,
        )

    x_started = []

    def x_go(slot, piece, xx):
        copy = x_copy(slot, piece, len(x_started), xx)
        copy.start()
        x_started.append(copy)

    def x_here(slot, piece):
        x_copy(slot, piece, 0, right).wait_recv()

    def own_go():
        for piece in range(PIECES):
            z_copy(c, piece, 0, beside).start()
            x_go(c, piece, right)
            pl.when(jnp.logical_not(end))(lambda piece=piece: z_copy(c, piece, 1, middle).start())
            x_go(c, (piece + PIECES // 2) % PIECES, left)

    def along(i, piece):
        slot = x * 4 + order[i]
        z_copy(slot, piece, 0, beside).wait_recv()
        onward = middle if i == 1 else beside
        pl.when(jnp.logical_not(end))(lambda: z_copy(slot, piece, 1 + i, onward).start())
        x_go(slot, piece, right)
        x_go(slot, piece, left)

    def pass_on(i, piece):
        if piece < PIECES // 2:
            slot, onward = left * 4 + order[i], right
        else:
            slot, onward = right * 4 + order[i], left
        x_here(slot, piece)
        x_go(slot, piece, onward)

    place = dict(own=x, left=left, right=right, across=across)

    def multiply(i, sides):
        for piece in range(PIECES):
            if 'left' in sides and piece >= PIECES // 2:
                x_here(left * 4 + order[i], piece)
            if 'right' in sides and piece < PIECES // 2:
                x_here(right * 4 + order[i], piece)
            if 'across' in sides:
                x_here(across * 4 + order[i], piece)

        def block(at, _):
            at = pl.ds(pl.multiple_of(at * 256, 256), 256)
            value = acc[at]
            for side in sides:
                slot = place[side] * 4 + order[i]
                rows = w_all[pl.ds(2 * slot, 2)].reshape(chans, -1)
                value = value + jnp.dot(g_all[slot, at], rows, preferred_element_type=F32)
            acc[at] = value
            return 0

        lax.fori_loop(0, tokens // 256, block, 0)

    def w_other(at, _):
        w_here(at * 2 + 1 - k)
        return 0

    own_go()
    w_chain(True, 2)
    w_chain(False, 1)
    along(1, 0)
    along(1, 1)
    pass_on(0, 0)
    pass_on(0, 2)
    along(2, 0)
    pass_on(0, 1)
    pass_on(0, 3)
    along(1, 2)
    along(2, 1)
    along(1, 3)
    along(2, 2)
    along(2, 3)
    w_chain(True, 3)
    w_chain(False, 2)
    for piece in range(PIECES):
        along(3, piece)
    for piece in (0, 2, 1, 3):
        pass_on(1, piece)
    w_chain(True, 4)
    w_chain(False, 3)
    for piece in (0, 2, 1, 3):
        pass_on(2, piece)
    w_chain(False, 4)
    lax.fori_loop(0, 16, w_other, 0)
    everyone = tuple(place)
    multiply(0, everyone)
    multiply(1, everyone)
    for piece in (0, 2, 1, 3):
        pass_on(3, piece)
    multiply(2, everyone)
    multiply(3, ('own', 'left', 'right'))
    multiply(3, ('across',))
    out[...] = acc[...].astype(BF16)

    for copy in x_started + w_started:
        copy.wait_send()
    for piece in range(PIECES):
        z_copy(c, piece, 0, beside).wait_send()

    @pl.when(jnp.logical_not(end))
    def _():
        for at in range(1, 5):
            for piece in range(PIECES):
                z_copy(c, piece, at, beside).wait_send()

    def msg_gone(step, _):
        msg_copy(h, k, step, s).wait_send()
        return 0

    def half_gone(j, _):
        msg_copy(j, k, 16 + j, partner).wait_send()
        return 0

    lax.fori_loop(0, h, half_gone, 0)

    lax.fori_loop(1, 16 - h, msg_gone, 0)


def body(projected, short_w, residues, rates, skip, w_out):
    tokens, _, chans = projected.shape
    rows, feats = w_out.shape
    length = tokens * lax.axis_size("seq")
    tiles, steps = chans // LANES, tokens // SUBS
    vmem = pl.BlockSpec(memory_space=pltpu.VMEM)
    dma = pltpu.SemaphoreType.DMA
    return pl.pallas_call(
        functools.partial(kernel, length),
        out_shape=jax.ShapeDtypeStruct((tokens, feats), BF16),
        in_specs=[pl.BlockSpec(memory_space=pltpu.HBM)] * 6,
        out_specs=vmem,
        scratch_shapes=[
            pltpu.VMEM((3, tokens, chans), BF16),
            pltpu.VMEM((3, 3, chans), F32),
            pltpu.VMEM((MODES, chans), F32),
            pltpu.VMEM((MODES, chans), F32),
            pltpu.VMEM((1, chans), F32),
            pltpu.VMEM((3, tiles, 8 + tokens, LANES), F32),
            pltpu.VMEM((MODES, chans), F32),
            pltpu.VMEM((4, MODES, chans), F32),
            pltpu.VMEM((MODES, SUBS, chans), F32),
            pltpu.VMEM((steps, SUBS, chans), F32),
            pltpu.VMEM((steps, SUBS, chans), F32),
            pltpu.VMEM((steps, SUBS, chans), F32),
            pltpu.VMEM((MODES, SUBS, chans), F32),
            pltpu.VMEM((MODES, chans), F32),
            pltpu.VMEM((2, 32, chans), BF16),
            pltpu.VMEM((16, 2, 16, chans), BF16),
            pltpu.VMEM((tiles, 17 * 16, LANES), F32),
            pltpu.VMEM((2, 16, chans), F32),
            pltpu.VMEM((tiles, tokens, LANES), F32),
            pltpu.VMEM((16, tokens, chans), BF16),
            pltpu.VMEM((32, rows, feats), BF16),
            pltpu.VMEM((tokens, feats), F32),
            dma((6,)),
            dma((2,)),
            dma((32,)),
            dma((16, 2)),
            dma((32,)),
            dma((32,)),
            dma((5, PIECES)),
            dma((4, PIECES)),
            dma((12 * PIECES,)),
            dma((16, PIECES)),
        ],
        compiler_params=pltpu.CompilerParams(
            collective_id=0, has_side_effects=True, vmem_limit_bytes=63 << 20
        ),
        cost_estimate=pl.CostEstimate(flops=2 * tokens * feats * 4096, bytes_accessed=4 << 20, transcendentals=0),
    )(projected.transpose(1, 0, 2), short_w, residues.T, rates.T, skip.reshape(1, chans), w_out)


def solution(mesh):
    return jax.shard_map(
        body,
        mesh=mesh,
        in_specs=(
            P("seq", None, "chan"),
            P(None, None, "chan"),
            P("chan", None),
            P("chan", None),
            P("chan"),
            P("seq", "chan"),
        ),
        out_specs=P("seq", "chan"),
        check_vma=False,
    )
```

```python
import functools

import jax
import jax.numpy as jnp
from jax import lax
from jax.experimental import pallas as pl
from jax.experimental.pallas import tpu as pltpu
from jax.sharding import PartitionSpec as P

MESH = pl.DeviceIdType.MESH
MODES = 16
SUBS = 8
LANES = 128
PIECES = 4
F32, BF16 = jnp.float32, jnp.bfloat16


def rounded(value):
    return value.astype(BF16).astype(F32)


def total_of(terms):
    terms = list(terms)
    while len(terms) > 1:
        terms = [a + b for a, b in zip(terms[::2], terms[1::2])] + terms[len(terms) // 2 * 2 :]
    return terms[0]


def kernel(
    length,
    proj_hbm,
    short_hbm,
    res_hbm,
    rate_hbm,
    skip_hbm,
    w_hbm,
    out,
    proj,
    short_w,
    res,
    rate,
    skip,
    wide,
    coef,
    dec,
    sub_dec,
    u_buf,
    q_buf,
    y_buf,
    part,
    own_total,
    pair,
    msg,
    edges,
    firsts,
    g_wide,
    g_all,
    w_all,
    acc,
    result,
    load_sem,
    pair_sem,
    msg_send,
    msg_recv,
    w_send,
    w_recv,
    z_send,
    z_recv,
    x_send,
    x_recv,
):
    s = lax.axis_index("seq")
    c = lax.axis_index("chan")
    y, zh, k = s // 4, (s // 2) % 2, s % 2
    x, zl = c // 4, c % 4
    h = s // 2
    tokens, chans = proj.shape[1], proj.shape[2]
    tiles = chans // LANES
    steps = tokens // SUBS
    half = tokens // 2

    def seq_of(yy, zz, kk):
        return yy * 4 + zz * 2 + kk

    up_y, down_y = (y + 1) % 8, (y + 7) % 8
    right, left, across = (x + 1) % 4, (x + 3) % 4, (x + 2) % 4
    partner = seq_of(y, zh, 1 - k)

    loads = []
    for at, (source, target) in enumerate(
        ((rate_hbm, rate), (res_hbm, res), (short_hbm, short_w), (skip_hbm, skip), (proj_hbm, proj), (w_hbm, w_all.at[s]))
    ):
        loads.append(pltpu.make_async_copy(source, target, load_sem.at[at]))
        loads[-1].start()

    barrier = pltpu.get_barrier_semaphore()

    def greet(seq, chan):
        pl.semaphore_signal(barrier, inc=1, device_id=(seq, chan), device_id_type=MESH)

    greet(partner, c)
    for step in (1, 3):
        greet(s, (x + step) % 4 * 4 + zl)
        greet(s, x * 4 + (zl + step) % 4)

    def greet_chip(step, _):
        greet((h + step) % 16 * 2 + k, c)
        return 0

    lax.fori_loop(1, 16, greet_chip, 0)

    acc[...] = jnp.zeros_like(acc)
    edges[...] = jnp.zeros_like(edges)

    for copy in loads[:4]:
        copy.wait()
    speed = rate[...] * (1.0 / length)
    scale = res[...] * jnp.sqrt(2.0 * rate[...] * (1.0 / length))
    coef[...] = scale

    def decay(count):
        return jnp.exp(speed * (-1.0 * count))

    for at, count in enumerate((1, steps, 2 * steps, 4 * steps)):
        dec[at] = decay(count)
    sub = lax.broadcasted_iota(jnp.int32, (SUBS, chans), 0)
    sub_steps = sub.astype(F32) * (-1.0 * steps)
    for m in range(MODES):
        sub_dec[m] = jnp.exp(jnp.broadcast_to(speed[m : m + 1], (SUBS, chans)) * sub_steps)

    loads[4].wait()
    for stream in range(3):
        for tile in range(tiles):
            lanes = pl.ds(tile * LANES, LANES)
            wide[stream, tile, 0:8, :] = jnp.zeros((8, LANES), F32)
            wide[stream, tile, 8 : 8 + tokens, :] = proj[stream, :, lanes].astype(F32)

    sub1 = lax.broadcasted_iota(jnp.int32, (SUBS, LANES), 0)
    keep = jnp.where((sub1 > 0) | (s == 0), 1.0, 0.0).astype(F32)

    def row(ref, lanes, *index):
        return jnp.broadcast_to(ref[index + (lanes,)], (SUBS, LANES))

    for tile in range(tiles):
        lanes = pl.ds(tile * LANES, LANES)
        taps = [[row(short_w, lanes, j, slice(st, st + 1)) for j in range(3)] for st in range(3)]
        skip_row = row(skip, lanes, slice(0, 1))

        def rows_at(stream, start, tile=tile):
            return wide[stream, tile, pl.ds(start, SUBS, stride=steps), :]

        def scan_step(i, carry, first=False, tile=tile, lanes=lanes, taps=taps, skip_row=skip_row):
            state, behind = carry
            feats, now = [], []
            for st in range(3):
                value = rows_at(st, 8 + i)
                one, two = behind[st]
                feats.append(taps[st][0] * value + taps[st][1] * one + taps[st][2] * two)
                now.append((value, one))
            u = rounded(feats[1] * feats[2])
            if first:
                u = u * keep
            state = tuple(
                row(dec, lanes, 0, slice(m, m + 1)) * state[m] + row(coef, lanes, slice(m, m + 1)) * u
                for m in range(MODES)
            )
            q_buf[i, :, lanes] = rounded(feats[0])
            u_buf[i, :, lanes] = u
            y_buf[i, :, lanes] = total_of(state) + skip_row * u
            return state, tuple(now)

        carry = (
            tuple(jnp.zeros((SUBS, LANES), F32) for _ in range(MODES)),
            tuple((rows_at(st, 7), rows_at(st, 6)) for st in range(3)),
        )
        carry = scan_step(0, carry, True)
        carry = scan_step(1, carry, True)
        state, _ = lax.fori_loop(2, steps, scan_step, carry)
        for m in range(MODES):
            value = state[m]
            for at, shift in ((1, 1), (2, 2), (3, 4)):
                moved = pltpu.roll(value, shift, 0)
                value = value + row(dec, lanes, at, slice(m, m + 1)) * jnp.where(sub1 >= shift, moved, 0.0)
            own_total[m : m + 1, lanes] = value[SUBS - 1 : SUBS]
            part[m, :, lanes] = jnp.where(sub1 >= 1, pltpu.roll(value, 1, 0), 0.0)

    def ends(stream, first):
        start = 0 if first else tokens - 2
        return jnp.concatenate([wide[stream, t, pl.ds(8 + start, 2), :] for t in range(tiles)], axis=1)

    mine = [own_total[...]]
    mine += [ends(1, True), ends(2, True), ends(1, False), ends(2, False), ends(0, False)]
    mine += [jnp.zeros((6, chans), F32)]
    pair[0] = jnp.concatenate(mine, axis=0).astype(BF16)

    pl.semaphore_wait(barrier, 20)

    pair_copy = pltpu.make_async_remote_copy(
        src_ref=pair.at[0], dst_ref=pair.at[1], send_sem=pair_sem.at[0], recv_sem=pair_sem.at[1],
        device_id=(partner, c), device_id_type=MESH,
    )
    pair_copy.start()

    def w_copy(slot, at, seq):
        return pltpu.make_async_remote_copy(
            src_ref=w_all.at[slot], dst_ref=w_all.at[slot], send_sem=w_send.at[at], recv_sem=w_recv.at[slot],
            device_id=(seq, c), device_id_type=MESH,
        )

    w_started = []

    def w_go(slot, seq):
        copy = w_copy(slot, len(w_started), seq)
        copy.start()
        w_started.append(copy)

    def w_here(slot):
        w_copy(slot, 0, partner).wait_recv()

    pair_copy.wait()

    def short(stream, two, one, zero):
        w0, w1, w2 = (short_w[j, stream : stream + 1, :] for j in range(3))
        return w0 * zero + w1 * one + w2 * two

    def edge(last, first, streams):
        gives = []
        for stream, before, own in zip(streams, last, first):
            gives.append(
                (
                    short(stream, before[0:1], before[1:2], own[0:1]),
                    short(stream, before[1:2], own[0:1], own[1:2]),
                )
            )
        return gives

    def edge_inner(last, first):
        (k0, k1), (v0, v1) = edge(last, first, (1, 2))
        return rounded(k0 * v0), rounded(k1 * v1)

    own_t, other_t = own_total[...], pair[1, 0:16, :].astype(F32)
    own_edges, other_edges = pair[0, 16:32, :].astype(F32), pair[1, 16:32, :].astype(F32)
    low = k == 0
    t_low, t_high = jnp.where(low, own_t, other_t), jnp.where(low, other_t, own_t)
    e_low, e_high = jnp.where(low, own_edges, other_edges), jnp.where(low, other_edges, own_edges)
    m0, m1 = edge_inner((e_low[4:6], e_low[6:8]), (e_high[0:2], e_high[2:4]))
    chip_total = decay(tokens) * t_low + t_high + scale * (decay(tokens - 1) * m0 + decay(tokens - 2) * m1)
    for at, parts in enumerate(
        (
            (chip_total[0:8], e_low[0:4], jnp.zeros((4, chans), F32)),
            (chip_total[8:16], e_high[4:10], jnp.zeros((2, chans), F32)),
        )
    ):
        msg[h, at] = jnp.concatenate(parts, axis=0).astype(BF16)

    def msg_copy(slot, part_at, step, seq):
        return pltpu.make_async_remote_copy(
            src_ref=msg.at[slot, part_at], dst_ref=msg.at[slot, part_at], send_sem=msg_send.at[step],
            recv_sem=msg_recv.at[slot, part_at], device_id=(seq, c), device_id_type=MESH,
        )

    def msg_go(step, _):
        msg_copy(h, k, step, (h + step) * 2 + k).start()
        return 0

    lax.fori_loop(1, 16 - h, msg_go, 0)

    def w_chain(own, n):
        zz, ups, downs = (zh, 4, 3) if own else (other_z, 3, 4)
        if n == 0:
            slot = seq_of(y, zz, k)
            w_here(slot)
            w_go(slot, seq_of(up_y, zh, k))
            w_go(slot, seq_of(down_y, zh, k))
            w_go(slot, partner)
            return
        for here, limit, onward in (((y + 8 - n) % 8, ups, up_y), ((y + n) % 8, downs, down_y)):
            if n <= limit:
                slot = seq_of(here, zz, k)
                w_here(slot)
                if n < limit:
                    w_go(slot, seq_of(onward, zh, k))
                w_go(slot, partner)

    loads[5].wait()
    other_z = 1 - zh
    w_go(s, seq_of(y, other_z, k))
    w_go(s, seq_of(up_y, zh, k))
    w_go(s, seq_of(down_y, zh, k))
    w_go(s, partner)

    far = decay(2 * tokens)
    far1, far2 = scale * decay(2 * tokens - 1), scale * decay(2 * tokens - 2)

    def put_edges(j):
        for at in range(2):
            values = msg[j, at].astype(F32)[8:16]
            for tile in range(tiles):
                edges[tile, pl.ds(j * 16 + 16 + 8 * at, 8), :] = values[:, tile * LANES : tile * LANES + LANES]

    def half_here(j, _):
        msg_copy(j, k, 0, s).wait_recv()
        msg_copy(j, k, 16 + j, partner).start()
        return 0

    def chip_here(j, _):
        msg_copy(j, 1 - k, 0, s).wait_recv()
        put_edges(j)
        return 0

    put_edges(h)
    w_chain(True, 1)
    lax.fori_loop(0, h, half_here, 0)
    w_chain(False, 0)
    lax.fori_loop(0, h, chip_here, 0)
    for tile in range(tiles):
        lanes = pl.ds(tile * LANES, LANES)

        def taps_of(stream, lanes=lanes):
            return [jnp.broadcast_to(short_w[j, stream : stream + 1, lanes], (16, LANES)) for j in range(3)]

        def edge_rows(at, before, tile=tile):
            return edges[tile, pl.ds(at + (0 if before else 16), 16, stride=16), :]

        (k0, k1), (v0, v1) = (
            (
                w0 * edge_rows(2 * st, False) + w1 * edge_rows(9 + 2 * st, True) + w2 * edge_rows(8 + 2 * st, True),
                w0 * edge_rows(2 * st + 1, False) + w1 * edge_rows(2 * st, False) + w2 * edge_rows(9 + 2 * st, True),
            )
            for st, (w0, w1, w2) in enumerate((taps_of(1), taps_of(2)))
        )
        firsts[0, :, lanes] = rounded(k0 * v0)
        firsts[1, :, lanes] = rounded(k1 * v1)

    def add_chip(j, state):
        after = jnp.where(j == 0, 0.0, 1.0)
        u0, u1 = firsts[0, pl.ds(j, 1), :], firsts[1, pl.ds(j, 1), :]
        total = jnp.concatenate([msg[j, at].astype(F32)[0:8] for at in range(2)], axis=0)
        return far * state + total + after * (far1 * u0 + far2 * u1)

    chip_in = lax.fori_loop(0, h, add_chip, jnp.zeros((MODES, chans), F32))
    f0, f1 = firsts[0, pl.ds(h, 1), :], firsts[1, pl.ds(h, 1), :]
    chip_first = jnp.where(h == 0, 0.0, 1.0)
    chip_last_q = jnp.concatenate([edges[tile, pl.ds(h * 16 + 12, 2), :] for tile in range(tiles)], axis=1)
    high_in = decay(tokens) * chip_in + t_low
    high_in += chip_first * scale * (decay(tokens - 1) * f0 + decay(tokens - 2) * f1)
    state_in = jnp.where(low, chip_in, high_in)
    u_first = (jnp.where(low, f0 * chip_first, m0), jnp.where(low, f1 * chip_first, m1))
    first_in = scale * (decay(steps - 1) * u_first[0] + decay(steps - 2) * u_first[1])
    q_last = jnp.where(low, chip_last_q, e_low[8:10])
    q_first = edge((q_last,), (ends(0, True),), (0,))[0]

    end = (zl == 0) | (zl == 3)
    beside = x * 4 + zl + 1 - 2 * (zl % 2)
    middle = x * 4 + 3 - zl
    order = (zl, zl + 1 - 2 * (zl % 2), 2 - zl // 2, 3 - 3 * (zl // 2))

    def z_copy(slot, piece, at, chan):
        ref = g_all.at[slot, piece // 2, pl.ds(piece % 2 * half, half)]
        return pltpu.make_async_remote_copy(
            src_ref=ref, dst_ref=ref, send_sem=z_send.at[at, piece],
            recv_sem=z_recv.at[slot % 4, piece], device_id=(s, chan), device_id_type=MESH,
        )

    def x_copy(slot, piece, at, xx):
        ref = g_all.at[slot, piece // 2, pl.ds(piece % 2 * half, half)]
        return pltpu.make_async_remote_copy(
            src_ref=ref, dst_ref=ref, send_sem=x_send.at[at],
            recv_sem=x_recv.at[slot, piece], device_id=(s, xx * 4 + zl), device_id_type=MESH,
        )

    x_started = []

    def x_go(slot, piece, xx):
        copy = x_copy(slot, piece, len(x_started), xx)
        copy.start()
        x_started.append(copy)

    def x_here(slot, piece):
        x_copy(slot, piece, 0, right).wait_recv()

    def own_go(tile):
        for piece, other in ((2 * tile, 2 * tile + 1), (2 * tile + 1, 2 * tile)):
            z_copy(c, piece, 0, beside).start()
            x_go(c, piece, right)
            pl.when(jnp.logical_not(end))(lambda piece=piece: z_copy(c, piece, 1, middle).start())
            x_go(c, other, left)

    def along(i, piece):
        slot = x * 4 + order[i]
        z_copy(slot, piece, 0, beside).wait_recv()
        onward = middle if i == 1 else beside
        pl.when(jnp.logical_not(end))(lambda: z_copy(slot, piece, 1 + i, onward).start())
        x_go(slot, piece, right)
        x_go(slot, piece, left)

    def pass_on(i, piece):
        if piece % 2 == 0:
            slot, onward = left * 4 + order[i], right
        else:
            slot, onward = right * 4 + order[i], left
        x_here(slot, piece)
        x_go(slot, piece, onward)

    for tile in range(tiles):
        cut = slice(tile * LANES, tile * LANES + LANES)
        lanes = pl.ds(tile * LANES, LANES)
        skip_row = row(skip, lanes, slice(0, 1))
        state = []
        for m in range(MODES):
            fade = sub_dec[m, :, lanes]
            after = jnp.where(sub1 >= 1, pltpu.roll(fade, 1, 0), 0.0)
            state.append(
                part[m, :, lanes]
                + fade * jnp.broadcast_to(state_in[m : m + 1, cut], (SUBS, LANES))
                + after * jnp.broadcast_to(first_in[m : m + 1, cut], (SUBS, LANES))
            )
        state = tuple(state)

        def gate_step(i, state, first=None, lanes=lanes, tile=tile, cut=cut, skip_row=skip_row):
            state = tuple(row(dec, lanes, 0, slice(m, m + 1)) * state[m] for m in range(MODES))
            conv, q = y_buf[i, :, lanes], q_buf[i, :, lanes]
            if first is not None:
                u = jnp.where(sub1 == 0, jnp.broadcast_to(u_first[first][:, cut], (SUBS, LANES)), 0.0)
                state = tuple(state[m] + row(coef, lanes, slice(m, m + 1)) * u for m in range(MODES))
                conv = conv + skip_row * u
                q = jnp.where(sub1 == 0, jnp.broadcast_to(rounded(q_first[first][:, cut]), (SUBS, LANES)), q)
            conv = rounded(conv + total_of(state))
            g_wide[tile, pl.ds(i, SUBS, stride=steps), :] = q * conv
            return state

        state = gate_step(0, state, 0)
        state = gate_step(1, state, 1)
        lax.fori_loop(2, steps, gate_step, state)
        g_all[c, tile] = g_wide[tile].astype(BF16)
        own_go(tile)

    place = dict(own=x, left=left, right=right, across=across)

    def arrived(i, sides, odd):
        for piece in (odd, 2 + odd):
            if 'left' in sides and odd:
                x_here(left * 4 + order[i], piece)
            if 'right' in sides and not odd:
                x_here(right * 4 + order[i], piece)
            if 'across' in sides:
                x_here(across * 4 + order[i], piece)

    def products(i, sides, at):
        value = acc[at]
        for side in sides:
            slot = place[side] * 4 + order[i]
            rows = w_all[pl.ds(2 * slot, 2)].reshape(chans, -1)
            left_side = jnp.concatenate([g_all[slot, tile, at] for tile in range(tiles)], axis=1)
            value = value + jnp.dot(left_side, rows, preferred_element_type=F32)
        return value

    def multiply(i, sides):
        for odd in range(2):
            arrived(i, sides, odd)

        def block(at, _):
            at = pl.ds(pl.multiple_of(at * half, half), half)
            acc[at] = products(i, sides, at)
            return 0

        lax.fori_loop(0, 2, block, 0)

    def w_other(at, _):
        w_here(at * 2 + 1 - k)
        return 0

    w_chain(True, 2)
    w_chain(False, 1)
    along(1, 0)
    along(1, 1)
    pass_on(0, 0)
    pass_on(0, 1)
    along(2, 0)
    pass_on(0, 2)
    pass_on(0, 3)
    along(1, 2)
    along(2, 1)
    along(1, 3)
    along(2, 2)
    along(2, 3)
    w_chain(True, 3)
    w_chain(False, 2)
    for piece in range(PIECES):
        along(3, piece)
    for piece in range(PIECES):
        pass_on(1, piece)
    w_chain(True, 4)
    w_chain(False, 3)
    for piece in range(PIECES):
        pass_on(2, piece)
    w_chain(False, 4)
    lax.fori_loop(0, 16, w_other, 0)
    everyone = tuple(place)
    multiply(0, everyone)
    multiply(1, everyone)
    for piece in range(PIECES):
        pass_on(3, piece)
    multiply(2, everyone)
    multiply(3, ('own', 'left', 'right'))
    out_copies = []
    for odd in range(2):
        at = pl.ds(odd * half, half)
        arrived(3, ('across',), odd)
        result[at] = products(3, ('across',), at).astype(BF16)
        out_copies.append(pltpu.make_async_copy(result.at[at], out.at[at], load_sem.at[odd]))
        out_copies[-1].start()

    for copy in x_started + w_started:
        copy.wait_send()
    for piece in range(PIECES):
        z_copy(c, piece, 0, beside).wait_send()

    @pl.when(jnp.logical_not(end))
    def _():
        for at in range(1, 5):
            for piece in range(PIECES):
                z_copy(c, piece, at, beside).wait_send()

    def msg_gone(step, _):
        msg_copy(h, k, step, s).wait_send()
        return 0

    def half_gone(j, _):
        msg_copy(j, k, 16 + j, partner).wait_send()
        return 0

    lax.fori_loop(0, h, half_gone, 0)

    lax.fori_loop(1, 16 - h, msg_gone, 0)
    for copy in out_copies:
        copy.wait()


def body(projected, short_w, residues, rates, skip, w_out):
    tokens, _, chans = projected.shape
    rows, feats = w_out.shape
    length = tokens * lax.axis_size("seq")
    tiles, steps = chans // LANES, tokens // SUBS
    dma = pltpu.SemaphoreType.DMA
    return pl.pallas_call(
        functools.partial(kernel, length),
        out_shape=jax.ShapeDtypeStruct((tokens, feats), BF16),
        in_specs=[pl.BlockSpec(memory_space=pltpu.HBM)] * 6,
        out_specs=pl.BlockSpec(memory_space=pltpu.HBM),
        scratch_shapes=[
            pltpu.VMEM((3, tokens, chans), BF16),
            pltpu.VMEM((3, 3, chans), F32),
            pltpu.VMEM((MODES, chans), F32),
            pltpu.VMEM((MODES, chans), F32),
            pltpu.VMEM((1, chans), F32),
            pltpu.VMEM((3, tiles, 8 + tokens, LANES), F32),
            pltpu.VMEM((MODES, chans), F32),
            pltpu.VMEM((4, MODES, chans), F32),
            pltpu.VMEM((MODES, SUBS, chans), F32),
            pltpu.VMEM((steps, SUBS, chans), F32),
            pltpu.VMEM((steps, SUBS, chans), F32),
            pltpu.VMEM((steps, SUBS, chans), F32),
            pltpu.VMEM((MODES, SUBS, chans), F32),
            pltpu.VMEM((MODES, chans), F32),
            pltpu.VMEM((2, 32, chans), BF16),
            pltpu.VMEM((16, 2, 16, chans), BF16),
            pltpu.VMEM((tiles, 17 * 16, LANES), F32),
            pltpu.VMEM((2, 16, chans), F32),
            pltpu.VMEM((tiles, tokens, LANES), F32),
            pltpu.VMEM((16, tiles, tokens, LANES), BF16),
            pltpu.VMEM((32, rows, feats), BF16),
            pltpu.VMEM((tokens, feats), F32),
            pltpu.VMEM((tokens, feats), BF16),
            dma((6,)),
            dma((2,)),
            dma((32,)),
            dma((16, 2)),
            dma((32,)),
            dma((32,)),
            dma((5, PIECES)),
            dma((4, PIECES)),
            dma((12 * PIECES,)),
            dma((16, PIECES)),
        ],
        compiler_params=pltpu.CompilerParams(
            collective_id=0, has_side_effects=True, vmem_limit_bytes=63 << 20
        ),
        cost_estimate=pl.CostEstimate(flops=2 * tokens * feats * 4096, bytes_accessed=4 << 20, transcendentals=0),
    )(projected.transpose(1, 0, 2), short_w, residues.T, rates.T, skip.reshape(1, chans), w_out)


def solution(mesh):
    return jax.shard_map(
        body,
        mesh=mesh,
        in_specs=(
            P("seq", None, "chan"),
            P(None, None, "chan"),
            P("chan", None),
            P("chan", None),
            P("chan"),
            P("seq", "chan"),
        ),
        out_specs=P("seq", "chan"),
        check_vma=False,
    )
```

```python
import functools

import jax
import jax.numpy as jnp
from jax import lax
from jax.experimental import pallas as pl
from jax.experimental.pallas import tpu as pltpu
from jax.sharding import PartitionSpec as P

MESH = pl.DeviceIdType.MESH
MODES = 16
SUBS = 8
LANES = 128
PIECES = 4
F32, BF16 = jnp.float32, jnp.bfloat16


def rounded(value):
    return value.astype(BF16).astype(F32)


def total_of(terms):
    terms = list(terms)
    while len(terms) > 1:
        terms = [a + b for a, b in zip(terms[::2], terms[1::2])] + terms[len(terms) // 2 * 2 :]
    return terms[0]


def kernel(
    length,
    proj_hbm,
    short_hbm,
    res_hbm,
    rate_hbm,
    skip_hbm,
    w_hbm,
    out,
    proj,
    short_w,
    res,
    rate,
    skip,
    wide,
    coef,
    dec,
    sub_dec,
    u_buf,
    q_buf,
    y_buf,
    part,
    own_total,
    pair,
    msg,
    edges,
    firsts,
    g_wide,
    g_all,
    w_all,
    acc,
    result,
    load_sem,
    pair_sem,
    msg_send,
    msg_recv,
    w_send,
    w_recv,
    z_send,
    z_recv,
    x_send,
    x_recv,
):
    s = lax.axis_index("seq")
    c = lax.axis_index("chan")
    y, zh, k = s // 4, (s // 2) % 2, s % 2
    x, zl = c // 4, c % 4
    h = s // 2
    tokens, chans = proj.shape[1], proj.shape[2]
    tiles = chans // LANES
    steps = tokens // SUBS
    half = tokens // 2

    def seq_of(yy, zz, kk):
        return yy * 4 + zz * 2 + kk

    up_y, down_y = (y + 1) % 8, (y + 7) % 8
    right, left, across = (x + 1) % 4, (x + 3) % 4, (x + 2) % 4
    partner = seq_of(y, zh, 1 - k)

    loads = []
    for at, (source, target) in enumerate(
        ((rate_hbm, rate), (res_hbm, res), (short_hbm, short_w), (skip_hbm, skip), (proj_hbm, proj), (w_hbm, w_all.at[s]))
    ):
        loads.append(pltpu.make_async_copy(source, target, load_sem.at[at]))
        loads[-1].start()

    barrier = pltpu.get_barrier_semaphore()

    def greet(seq, chan):
        pl.semaphore_signal(barrier, inc=1, device_id=(seq, chan), device_id_type=MESH)

    greet(partner, c)
    for step in (1, 3):
        greet(s, (x + step) % 4 * 4 + zl)
        greet(s, x * 4 + (zl + step) % 4)

    def greet_chip(step, _):
        greet((h + step) % 16 * 2 + k, c)
        return 0

    lax.fori_loop(1, 16, greet_chip, 0)

    acc[...] = jnp.zeros_like(acc)
    edges[...] = jnp.zeros_like(edges)

    for copy in loads[:4]:
        copy.wait()
    speed = rate[...] * (1.0 / length)
    scale = res[...] * jnp.sqrt(2.0 * rate[...] * (1.0 / length))
    coef[...] = scale

    def decay(count):
        return jnp.exp(speed * (-1.0 * count))

    for at, count in enumerate((1, steps, 2 * steps, 4 * steps)):
        dec[at] = decay(count)
    sub = lax.broadcasted_iota(jnp.int32, (SUBS, chans), 0)
    sub_steps = sub.astype(F32) * (-1.0 * steps)
    for m in range(MODES):
        sub_dec[m] = jnp.exp(jnp.broadcast_to(speed[m : m + 1], (SUBS, chans)) * sub_steps)

    loads[4].wait()
    for stream in range(3):
        for tile in range(tiles):
            lanes = pl.ds(tile * LANES, LANES)
            wide[stream, tile, 0:8, :] = jnp.zeros((8, LANES), F32)
            wide[stream, tile, 8 : 8 + tokens, :] = proj[stream, :, lanes].astype(F32)

    sub1 = lax.broadcasted_iota(jnp.int32, (SUBS, LANES), 0)
    keep = jnp.where((sub1 > 0) | (s == 0), 1.0, 0.0).astype(F32)

    def row(ref, lanes, *index):
        return jnp.broadcast_to(ref[index + (lanes,)], (SUBS, LANES))

    for tile in range(tiles):
        lanes = pl.ds(tile * LANES, LANES)
        taps = [[row(short_w, lanes, j, slice(st, st + 1)) for j in range(3)] for st in range(3)]
        skip_row = row(skip, lanes, slice(0, 1))

        def rows_at(stream, start, tile=tile):
            return wide[stream, tile, pl.ds(start, SUBS, stride=steps), :]

        def scan_step(i, carry, first=False, tile=tile, lanes=lanes, taps=taps, skip_row=skip_row):
            state, behind = carry
            feats, now = [], []
            for st in range(3):
                value = rows_at(st, 8 + i)
                one, two = behind[st]
                feats.append(taps[st][0] * value + taps[st][1] * one + taps[st][2] * two)
                now.append((value, one))
            u = rounded(feats[1] * feats[2])
            if first:
                u = u * keep
            state = tuple(
                row(dec, lanes, 0, slice(m, m + 1)) * state[m] + row(coef, lanes, slice(m, m + 1)) * u
                for m in range(MODES)
            )
            q_buf[i, :, lanes] = rounded(feats[0])
            u_buf[i, :, lanes] = u
            y_buf[i, :, lanes] = total_of(state) + skip_row * u
            return state, tuple(now)

        carry = (
            tuple(jnp.zeros((SUBS, LANES), F32) for _ in range(MODES)),
            tuple((rows_at(st, 7), rows_at(st, 6)) for st in range(3)),
        )
        carry = scan_step(0, carry, True)
        carry = scan_step(1, carry, True)
        state, _ = lax.fori_loop(2, steps, scan_step, carry)
        for m in range(MODES):
            value = state[m]
            for at, shift in ((1, 1), (2, 2), (3, 4)):
                moved = pltpu.roll(value, shift, 0)
                value = value + row(dec, lanes, at, slice(m, m + 1)) * jnp.where(sub1 >= shift, moved, 0.0)
            own_total[m : m + 1, lanes] = value[SUBS - 1 : SUBS]
            part[m, :, lanes] = jnp.where(sub1 >= 1, pltpu.roll(value, 1, 0), 0.0)

    def ends(stream, first):
        start = 0 if first else tokens - 2
        return jnp.concatenate([wide[stream, t, pl.ds(8 + start, 2), :] for t in range(tiles)], axis=1)

    mine = [own_total[...]]
    mine += [ends(1, True), ends(2, True), ends(1, False), ends(2, False), ends(0, False)]
    mine += [jnp.zeros((6, chans), F32)]
    pair[0] = jnp.concatenate(mine, axis=0).astype(BF16)

    pl.semaphore_wait(barrier, 20)

    pair_copy = pltpu.make_async_remote_copy(
        src_ref=pair.at[0], dst_ref=pair.at[1], send_sem=pair_sem.at[0], recv_sem=pair_sem.at[1],
        device_id=(partner, c), device_id_type=MESH,
    )
    pair_copy.start()

    def w_copy(slot, at, seq):
        return pltpu.make_async_remote_copy(
            src_ref=w_all.at[slot], dst_ref=w_all.at[slot], send_sem=w_send.at[at], recv_sem=w_recv.at[slot],
            device_id=(seq, c), device_id_type=MESH,
        )

    w_started = []

    def w_go(slot, seq):
        copy = w_copy(slot, len(w_started), seq)
        copy.start()
        w_started.append(copy)

    def w_here(slot):
        w_copy(slot, 0, partner).wait_recv()

    pair_copy.wait()

    def short(stream, two, one, zero):
        w0, w1, w2 = (short_w[j, stream : stream + 1, :] for j in range(3))
        return w0 * zero + w1 * one + w2 * two

    def edge(last, first, streams):
        gives = []
        for stream, before, own in zip(streams, last, first):
            gives.append(
                (
                    short(stream, before[0:1], before[1:2], own[0:1]),
                    short(stream, before[1:2], own[0:1], own[1:2]),
                )
            )
        return gives

    def edge_inner(last, first):
        (k0, k1), (v0, v1) = edge(last, first, (1, 2))
        return rounded(k0 * v0), rounded(k1 * v1)

    own_t, other_t = own_total[...], pair[1, 0:16, :].astype(F32)
    own_edges, other_edges = pair[0, 16:32, :].astype(F32), pair[1, 16:32, :].astype(F32)
    low = k == 0
    t_low, t_high = jnp.where(low, own_t, other_t), jnp.where(low, other_t, own_t)
    e_low, e_high = jnp.where(low, own_edges, other_edges), jnp.where(low, other_edges, own_edges)
    m0, m1 = edge_inner((e_low[4:6], e_low[6:8]), (e_high[0:2], e_high[2:4]))
    chip_total = decay(tokens) * t_low + t_high + scale * (decay(tokens - 1) * m0 + decay(tokens - 2) * m1)
    for at, parts in enumerate(
        (
            (chip_total[0:8], e_low[0:4], jnp.zeros((4, chans), F32)),
            (chip_total[8:16], e_high[4:10], jnp.zeros((2, chans), F32)),
        )
    ):
        msg[h, at] = jnp.concatenate(parts, axis=0).astype(BF16)

    def msg_copy(slot, part_at, step, seq):
        return pltpu.make_async_remote_copy(
            src_ref=msg.at[slot, part_at], dst_ref=msg.at[slot, part_at], send_sem=msg_send.at[step],
            recv_sem=msg_recv.at[slot, part_at], device_id=(seq, c), device_id_type=MESH,
        )

    def msg_go(step, _):
        msg_copy(h, k, step, (h + step) * 2 + k).start()
        return 0

    lax.fori_loop(1, 16 - h, msg_go, 0)

    def w_chain(own, n):
        zz, ups, downs = (zh, 4, 3) if own else (other_z, 3, 4)
        if n == 0:
            slot = seq_of(y, zz, k)
            w_here(slot)
            w_go(slot, seq_of(up_y, zh, k))
            w_go(slot, seq_of(down_y, zh, k))
            w_go(slot, partner)
            return
        for here, limit, onward in (((y + 8 - n) % 8, ups, up_y), ((y + n) % 8, downs, down_y)):
            if n <= limit:
                slot = seq_of(here, zz, k)
                w_here(slot)
                if n < limit:
                    w_go(slot, seq_of(onward, zh, k))
                w_go(slot, partner)

    loads[5].wait()
    other_z = 1 - zh
    w_go(s, seq_of(y, other_z, k))
    w_go(s, seq_of(up_y, zh, k))
    w_go(s, seq_of(down_y, zh, k))
    w_go(s, partner)

    far = decay(2 * tokens)
    far1, far2 = scale * decay(2 * tokens - 1), scale * decay(2 * tokens - 2)

    def put_edges(j):
        for at in range(2):
            values = msg[j, at].astype(F32)[8:16]
            for tile in range(tiles):
                edges[tile, pl.ds(j * 16 + 16 + 8 * at, 8), :] = values[:, tile * LANES : tile * LANES + LANES]

    def half_here(j, _):
        msg_copy(j, k, 0, s).wait_recv()
        msg_copy(j, k, 16 + j, partner).start()
        return 0

    def chip_here(j, _):
        msg_copy(j, 1 - k, 0, s).wait_recv()
        put_edges(j)
        return 0

    put_edges(h)
    w_chain(True, 1)
    lax.fori_loop(0, h, half_here, 0)
    w_chain(False, 0)
    lax.fori_loop(0, h, chip_here, 0)
    for tile in range(tiles):
        lanes = pl.ds(tile * LANES, LANES)

        def taps_of(stream, lanes=lanes):
            return [jnp.broadcast_to(short_w[j, stream : stream + 1, lanes], (16, LANES)) for j in range(3)]

        def edge_rows(at, before, tile=tile):
            return edges[tile, pl.ds(at + (0 if before else 16), 16, stride=16), :]

        (k0, k1), (v0, v1) = (
            (
                w0 * edge_rows(2 * st, False) + w1 * edge_rows(9 + 2 * st, True) + w2 * edge_rows(8 + 2 * st, True),
                w0 * edge_rows(2 * st + 1, False) + w1 * edge_rows(2 * st, False) + w2 * edge_rows(9 + 2 * st, True),
            )
            for st, (w0, w1, w2) in enumerate((taps_of(1), taps_of(2)))
        )
        firsts[0, :, lanes] = rounded(k0 * v0)
        firsts[1, :, lanes] = rounded(k1 * v1)

    def add_chip(j, state):
        after = jnp.where(j == 0, 0.0, 1.0)
        u0, u1 = firsts[0, pl.ds(j, 1), :], firsts[1, pl.ds(j, 1), :]
        total = jnp.concatenate([msg[j, at].astype(F32)[0:8] for at in range(2)], axis=0)
        return far * state + total + after * (far1 * u0 + far2 * u1)

    chip_in = lax.fori_loop(0, h, add_chip, jnp.zeros((MODES, chans), F32))
    f0, f1 = firsts[0, pl.ds(h, 1), :], firsts[1, pl.ds(h, 1), :]
    chip_first = jnp.where(h == 0, 0.0, 1.0)
    chip_last_q = jnp.concatenate([edges[tile, pl.ds(h * 16 + 12, 2), :] for tile in range(tiles)], axis=1)
    high_in = decay(tokens) * chip_in + t_low
    high_in += chip_first * scale * (decay(tokens - 1) * f0 + decay(tokens - 2) * f1)
    state_in = jnp.where(low, chip_in, high_in)
    u_first = (jnp.where(low, f0 * chip_first, m0), jnp.where(low, f1 * chip_first, m1))
    first_in = scale * (decay(steps - 1) * u_first[0] + decay(steps - 2) * u_first[1])
    q_last = jnp.where(low, chip_last_q, e_low[8:10])
    q_first = edge((q_last,), (ends(0, True),), (0,))[0]

    end = (zl == 0) | (zl == 3)
    beside = x * 4 + zl + 1 - 2 * (zl % 2)
    middle = x * 4 + 3 - zl
    order = (zl, zl + 1 - 2 * (zl % 2), 2 - zl // 2, 3 - 3 * (zl // 2))

    def z_copy(slot, piece, at, chan):
        ref = g_all.at[slot, piece // 2, pl.ds(piece % 2 * half, half)]
        return pltpu.make_async_remote_copy(
            src_ref=ref, dst_ref=ref, send_sem=z_send.at[at, piece],
            recv_sem=z_recv.at[slot % 4, piece], device_id=(s, chan), device_id_type=MESH,
        )

    def x_copy(slot, piece, at, xx):
        ref = g_all.at[slot, piece // 2, pl.ds(piece % 2 * half, half)]
        return pltpu.make_async_remote_copy(
            src_ref=ref, dst_ref=ref, send_sem=x_send.at[at],
            recv_sem=x_recv.at[slot, piece], device_id=(s, xx * 4 + zl), device_id_type=MESH,
        )

    x_started = []

    def x_go(slot, piece, xx):
        copy = x_copy(slot, piece, len(x_started), xx)
        copy.start()
        x_started.append(copy)

    def x_here(slot, piece):
        x_copy(slot, piece, 0, right).wait_recv()

    def own_go(tile):
        for piece, other in ((2 * tile, 2 * tile + 1), (2 * tile + 1, 2 * tile)):
            z_copy(c, piece, 0, beside).start()
            x_go(c, piece, right)
            pl.when(jnp.logical_not(end))(lambda piece=piece: z_copy(c, piece, 1, middle).start())
            x_go(c, other, left)

    def along(i, piece):
        slot = x * 4 + order[i]
        z_copy(slot, piece, 0, beside).wait_recv()
        onward = middle if i == 1 else beside
        pl.when(jnp.logical_not(end))(lambda: z_copy(slot, piece, 1 + i, onward).start())
        x_go(slot, piece, right)
        x_go(slot, piece, left)

    def pass_on(i, piece):
        if piece % 2 == 0:
            slot, onward = left * 4 + order[i], right
        else:
            slot, onward = right * 4 + order[i], left
        x_here(slot, piece)
        x_go(slot, piece, onward)

    for tile in range(tiles):
        cut = slice(tile * LANES, tile * LANES + LANES)
        lanes = pl.ds(tile * LANES, LANES)
        skip_row = row(skip, lanes, slice(0, 1))
        state = []
        for m in range(MODES):
            fade = sub_dec[m, :, lanes]
            after = jnp.where(sub1 >= 1, pltpu.roll(fade, 1, 0), 0.0)
            state.append(
                part[m, :, lanes]
                + fade * jnp.broadcast_to(state_in[m : m + 1, cut], (SUBS, LANES))
                + after * jnp.broadcast_to(first_in[m : m + 1, cut], (SUBS, LANES))
            )
        state = tuple(state)

        def gate_step(i, state, first=None, lanes=lanes, tile=tile, cut=cut, skip_row=skip_row):
            state = tuple(row(dec, lanes, 0, slice(m, m + 1)) * state[m] for m in range(MODES))
            conv, q = y_buf[i, :, lanes], q_buf[i, :, lanes]
            if first is not None:
                u = jnp.where(sub1 == 0, jnp.broadcast_to(u_first[first][:, cut], (SUBS, LANES)), 0.0)
                state = tuple(state[m] + row(coef, lanes, slice(m, m + 1)) * u for m in range(MODES))
                conv = conv + skip_row * u
                q = jnp.where(sub1 == 0, jnp.broadcast_to(rounded(q_first[first][:, cut]), (SUBS, LANES)), q)
            conv = rounded(conv + total_of(state))
            g_wide[tile, pl.ds(i, SUBS, stride=steps), :] = q * conv
            return state

        state = gate_step(0, state, 0)
        state = gate_step(1, state, 1)
        lax.fori_loop(2, steps, gate_step, state)
        g_all[c, tile] = g_wide[tile].astype(BF16)
        own_go(tile)

    place = dict(own=x, left=left, right=right, across=across)

    def arrived(i, sides, odd):
        for piece in (odd, 2 + odd):
            if 'left' in sides and odd:
                x_here(left * 4 + order[i], piece)
            if 'right' in sides and not odd:
                x_here(right * 4 + order[i], piece)
            if 'across' in sides:
                x_here(across * 4 + order[i], piece)

    def products(i, sides, at):
        value = acc[at]
        for side in sides:
            slot = place[side] * 4 + order[i]
            rows = w_all[pl.ds(2 * slot, 2)].reshape(chans, -1)
            left_side = jnp.concatenate([g_all[slot, tile, at] for tile in range(tiles)], axis=1)
            value = value + jnp.dot(left_side, rows, preferred_element_type=F32)
        return value

    def multiply(i, sides):
        for odd in range(2):
            arrived(i, sides, odd)

        def block(at, _):
            at = pl.ds(pl.multiple_of(at * half, half), half)
            acc[at] = products(i, sides, at)
            return 0

        lax.fori_loop(0, 2, block, 0)

    def w_other(at, _):
        w_here(at * 2 + 1 - k)
        return 0

    w_chain(True, 2)
    w_chain(False, 1)
    along(1, 0)
    along(1, 1)
    pass_on(0, 0)
    pass_on(0, 1)
    along(2, 0)
    pass_on(0, 2)
    pass_on(0, 3)
    along(1, 2)
    along(2, 1)
    along(1, 3)
    along(2, 2)
    along(2, 3)
    w_chain(True, 3)
    w_chain(False, 2)
    for piece in range(PIECES):
        along(3, piece)
    for piece in range(PIECES):
        pass_on(1, piece)
    w_chain(True, 4)
    w_chain(False, 3)
    for piece in range(PIECES):
        pass_on(2, piece)
    w_chain(False, 4)
    lax.fori_loop(0, 16, w_other, 0)
    everyone = tuple(place)
    multiply(0, everyone)
    multiply(1, everyone)
    for piece in range(PIECES):
        pass_on(3, piece)
    multiply(2, everyone)
    multiply(3, ('own', 'left', 'right'))
    far_slot = across * 4 + order[3]
    far_rows = w_all.at[pl.ds(2 * far_slot, 2)]
    for odd in range(2):
        at = pl.ds(odd * half, half)
        x_here(far_slot, odd)
        acc[at] += jnp.dot(g_all[far_slot, 0, at], far_rows[0], preferred_element_type=F32)
    out_copies = []
    for odd in range(2):
        at = pl.ds(odd * half, half)
        x_here(far_slot, 2 + odd)
        last = jnp.dot(g_all[far_slot, 1, at], far_rows[1], preferred_element_type=F32)
        result[at] = (acc[at] + last).astype(BF16)
        out_copies.append(pltpu.make_async_copy(result.at[at], out.at[at], load_sem.at[odd]))
        out_copies[-1].start()

    for copy in x_started + w_started:
        copy.wait_send()
    for piece in range(PIECES):
        z_copy(c, piece, 0, beside).wait_send()

    @pl.when(jnp.logical_not(end))
    def _():
        for at in range(1, 5):
            for piece in range(PIECES):
                z_copy(c, piece, at, beside).wait_send()

    def msg_gone(step, _):
        msg_copy(h, k, step, s).wait_send()
        return 0

    def half_gone(j, _):
        msg_copy(j, k, 16 + j, partner).wait_send()
        return 0

    lax.fori_loop(0, h, half_gone, 0)

    lax.fori_loop(1, 16 - h, msg_gone, 0)
    for copy in out_copies:
        copy.wait()


def body(projected, short_w, residues, rates, skip, w_out):
    tokens, _, chans = projected.shape
    rows, feats = w_out.shape
    length = tokens * lax.axis_size("seq")
    tiles, steps = chans // LANES, tokens // SUBS
    dma = pltpu.SemaphoreType.DMA
    return pl.pallas_call(
        functools.partial(kernel, length),
        out_shape=jax.ShapeDtypeStruct((tokens, feats), BF16),
        in_specs=[pl.BlockSpec(memory_space=pltpu.HBM)] * 6,
        out_specs=pl.BlockSpec(memory_space=pltpu.HBM),
        scratch_shapes=[
            pltpu.VMEM((3, tokens, chans), BF16),
            pltpu.VMEM((3, 3, chans), F32),
            pltpu.VMEM((MODES, chans), F32),
            pltpu.VMEM((MODES, chans), F32),
            pltpu.VMEM((1, chans), F32),
            pltpu.VMEM((3, tiles, 8 + tokens, LANES), F32),
            pltpu.VMEM((MODES, chans), F32),
            pltpu.VMEM((4, MODES, chans), F32),
            pltpu.VMEM((MODES, SUBS, chans), F32),
            pltpu.VMEM((steps, SUBS, chans), F32),
            pltpu.VMEM((steps, SUBS, chans), F32),
            pltpu.VMEM((steps, SUBS, chans), F32),
            pltpu.VMEM((MODES, SUBS, chans), F32),
            pltpu.VMEM((MODES, chans), F32),
            pltpu.VMEM((2, 32, chans), BF16),
            pltpu.VMEM((16, 2, 16, chans), BF16),
            pltpu.VMEM((tiles, 17 * 16, LANES), F32),
            pltpu.VMEM((2, 16, chans), F32),
            pltpu.VMEM((tiles, tokens, LANES), F32),
            pltpu.VMEM((16, tiles, tokens, LANES), BF16),
            pltpu.VMEM((32, rows, feats), BF16),
            pltpu.VMEM((tokens, feats), F32),
            pltpu.VMEM((tokens, feats), BF16),
            dma((6,)),
            dma((2,)),
            dma((32,)),
            dma((16, 2)),
            dma((32,)),
            dma((32,)),
            dma((5, PIECES)),
            dma((4, PIECES)),
            dma((12 * PIECES,)),
            dma((16, PIECES)),
        ],
        compiler_params=pltpu.CompilerParams(
            collective_id=0, has_side_effects=True, vmem_limit_bytes=63 << 20
        ),
        cost_estimate=pl.CostEstimate(flops=2 * tokens * feats * 4096, bytes_accessed=4 << 20, transcendentals=0),
    )(projected.transpose(1, 0, 2), short_w, residues.T, rates.T, skip.reshape(1, chans), w_out)


def solution(mesh):
    return jax.shard_map(
        body,
        mesh=mesh,
        in_specs=(
            P("seq", None, "chan"),
            P(None, None, "chan"),
            P("chan", None),
            P("chan", None),
            P("chan"),
            P("seq", "chan"),
        ),
        out_specs=P("seq", "chan"),
        check_vma=False,
    )
```
